32 devices in a mesh: row: 4 (over z), col: 8 (over y, x, core).
Axes of the slice: x: 2, y: 2, z: 4, core: 2. Of those that a mesh axis runs over, the one named last changes fastest.
Arguments:
- inputs: bfloat16 [384, 6144], P('col', 'row'), may hold values from -6 to 6
- cotangent: bfloat16 [384, 6144], P('col', 'row'), may hold values from -4 to 4
- gate_pre: bfloat16 [384, 16384], P('row', 'col'), may hold values from -10 to 10
- up_pre: bfloat16 [384, 16384], P('row', 'col'), may hold values from -6 to 6
- gate_weight: bfloat16 [6144, 16384], P('row', 'col'), may hold values from -0.078125 to 0.078125
- up_weight: bfloat16 [6144, 16384], P('row', 'col'), may hold values from -0.078125 to 0.078125
- down_weight: bfloat16 [16384, 6144], P('col', 'row'), may hold values from -0.046875 to 0.046875
Outputs:
- input_grad: bfloat16 [384, 6144], P('col', 'row')
- gate_grad: bfloat16 [6144, 16384], P('row', 'col')
- up_grad: bfloat16 [6144, 16384], P('row', 'col')
- down_grad: bfloat16 [16384, 6144], P('col', 'row')
The draws below stay inside these ranges and needn't reach their ends.
All inputs are finite; a program needn't handle non-finite values.
Results may differ from the reference program's by a relative error of at most 0.033.
Values may be sent and summed in bfloat16 or wider, within the bound.
No kernel may reach another device: no remote copies, remote signals or barrier semaphores. Data moves between devices by JAX's collectives and lax.ppermute only.
A program may use at most 128 MiB of HBM per device.

```python
import jax
import jax.numpy as jnp
from jax import lax

D = 6144
FF = 16384
TOKENS = 384
N_ROW = 4
N_COL = 8


def steps_of(own_key, shape, pieces, smallest, high):
    loudness, own = 1.0, jax.random.fold_in(own_key, 6)
    for position, parts in pieces:
        heights = jnp.exp(jax.random.uniform(jax.random.fold_in(own, position), (parts,), jnp.float32, smallest / len(pieces), high / len(pieces)))
        loudness = loudness * jnp.repeat(heights, shape[position] // parts).reshape([-1 if axis == position else 1 for axis in range(len(shape))])
    return loudness


def bell_draw(rng, shape, spread, reach, pieces=(), held_as=jnp.bfloat16):
    loudness = steps_of(rng, shape, pieces, -0.22, 0.18) if pieces else 1.0
    entries = jax.random.normal(rng, shape, jnp.float32) * spread * loudness
    return jnp.minimum(jnp.maximum(entries, -reach), reach).astype(held_as)


def setup_inputs(seed: int = 0) -> dict:
    arg_keys = jax.random.split(jax.random.key(seed), 8)
    return {
        "inputs": bell_draw(arg_keys[0], (TOKENS, D), 1.0, 6.0, ((0, 8), (1, 4))),
        "cotangent": bell_draw(arg_keys[1], (TOKENS, D), 0.5, 4.0, ((0, 8), (1, 4))),
        "gate_pre": bell_draw(arg_keys[2], (TOKENS, FF), 2.0, 10.0, ((0, 4), (1, 8))),
        "up_pre": bell_draw(arg_keys[3], (TOKENS, FF), 1.0, 6.0, ((0, 4), (1, 8))),
        "gate_weight": bell_draw(arg_keys[4], (D, FF), D ** -0.5, 0.078125, ((0, 4), (1, 8))),
        "up_weight": bell_draw(arg_keys[5], (D, FF), D ** -0.5, 0.078125, ((0, 4), (1, 8))),
        "down_weight": bell_draw(arg_keys[6], (FF, D), FF ** -0.5, 0.046875, ((0, 8), (1, 4))),
    }


def reference(inputs, cotangent, gate_pre, up_pre, gate_weight, up_weight, down_weight):
    gate_value = gate_pre.astype(jnp.float32)
    up_value = up_pre.astype(jnp.float32)
    sigma = jax.nn.sigmoid(gate_value)
    silu_value = gate_value * sigma
    hidden = (silu_value * up_value).astype(jnp.bfloat16)

    feat_block = D // N_ROW

    def add_feature_block(total, index):
        start = (index * feat_block).astype(jnp.int32)
        cot_block = lax.dynamic_slice_in_dim(cotangent, start, feat_block, 1)
        down_block = lax.dynamic_slice_in_dim(down_weight, start, feat_block, 1)
        partial_sum = jnp.dot(cot_block, down_block.T, preferred_element_type=jnp.float32)
        return total + partial_sum.astype(jnp.bfloat16).astype(jnp.float32), None

    hidden_grad, _ = lax.scan(add_feature_block, jnp.zeros((TOKENS, FF), jnp.float32), jnp.arange(N_ROW, dtype=jnp.int32))

    gate_delta = (hidden_grad * up_value * sigma * (1.0 + gate_value * (1.0 - sigma))).astype(jnp.bfloat16)
    up_delta = (hidden_grad * silu_value).astype(jnp.bfloat16)
    down_grad = jnp.dot(hidden.T, cotangent, preferred_element_type=jnp.float32).astype(jnp.bfloat16)
    gate_grad = jnp.dot(inputs.T, gate_delta, preferred_element_type=jnp.float32).astype(jnp.bfloat16)
    up_grad = jnp.dot(inputs.T, up_delta, preferred_element_type=jnp.float32).astype(jnp.bfloat16)

    unit_block = FF // N_COL

    def add_unit_block(total, index):
        start = (index * unit_block).astype(jnp.int32)
        gate_part = lax.dynamic_slice_in_dim(gate_delta, start, unit_block, 1)
        up_part = lax.dynamic_slice_in_dim(up_delta, start, unit_block, 1)
        gate_w = lax.dynamic_slice_in_dim(gate_weight, start, unit_block, 1)
        up_w = lax.dynamic_slice_in_dim(up_weight, start, unit_block, 1)
        term = jnp.dot(gate_part, gate_w.T, preferred_element_type=jnp.float32)
        term = term + jnp.dot(up_part, up_w.T, preferred_element_type=jnp.float32)
        return total + term.astype(jnp.bfloat16).astype(jnp.float32), None

    input_sum, _ = lax.scan(add_unit_block, jnp.zeros((TOKENS, D), jnp.float32), jnp.arange(N_COL, dtype=jnp.int32))
    input_grad = input_sum.astype(jnp.bfloat16)
    return input_grad, gate_grad, up_grad, down_grad
```

```python
import functools

import jax
import jax.numpy as jnp
from jax import lax
from jax.experimental import pallas as pl
from jax.experimental.pallas import tpu as pltpu
from jax.sharding import PartitionSpec as P

F32 = jnp.float32
BF16 = jnp.bfloat16
MIB = 1024 * 1024
NO_COST = pl.CostEstimate(flops=0, bytes_accessed=0, transcendentals=0)
CHUNKS = 4


def contract(left, right, left_dim, right_dim):
    return lax.dot_general(
        left, right, (((left_dim,), (right_dim,)), ((), ())), preferred_element_type=F32
    )


def whole(shape):
    return pl.BlockSpec(shape, lambda *_: (0,) * len(shape))


def tile_of(size, most):
    tile = min(size, most)
    while size % tile:
        tile //= 2
    return tile


def after(value, *others):
    return lax.optimization_barrier((value, *others))[0]


def inward(places, n):
    return [pair for p in places for pair in ((p, p + 1), (n - 1 - p, n - 2 - p))]


def outward(places, n):
    return [(target, source) for source, target in inward(places, n)]


def across(n):
    return [(n // 2 - 1, n // 2), (n // 2, n // 2 - 1)]


def own_half(block, n):
    half = n // 2
    ins, outs = [block], [block]
    for step in range(1, half):
        if half == 2:
            met = lax.ppermute(block, "row", inward([0], n) + outward([0], n))
            ins.append(met)
            outs.append(met)
        else:
            ins.append(lax.ppermute(ins[-1], "row", inward(range(step - 1, half - 1), n)))
            outs.append(lax.ppermute(outs[-1], "row", outward(range(half - step), n)))
    return ins, outs


def sent_out(block, place, n):
    got = block
    for step in reversed(range(n // 2 - 1)):
        if step < n // 2 - 2:
            block = jnp.where(place == step + 1, got, block)
        got = lax.ppermute(block, "row", outward([step], n))
    return block, got


def cube_bits(n):
    bits, bit = [], 1
    while bit < n:
        bits.append(bit)
        bit *= 2
    return bits


def cube_gather(block, n):
    pieces = {0: block}
    for bit in reversed(cube_bits(n)):
        pairs = [(i, i ^ bit) for i in range(n)]
        for slot in list(pieces):
            pieces[slot | bit] = lax.ppermute(pieces[slot], "col", pairs)
    return [pieces[k] for k in range(n)]


def rows_at(start, rows):
    return pl.ds(pl.multiple_of(start, 16), rows)


def spread(pieces, col, which, target):
    for slot, piece in enumerate(pieces):
        rows = piece.shape[0] // 2
        block = piece[which * rows : (which + 1) * rows, :]
        target[rows_at(jnp.bitwise_xor(col, slot) * rows, rows), :] = block


def in_hbm(array):
    return pltpu.with_memory_space_constraint(array, pltpu.HBM)


def join_kernel(*refs):
    arrived = refs[-1]
    count = len(refs) // 3
    copies = []
    for number, block in enumerate(refs[: 2 * count]):
        rows = block.shape[0]
        target = refs[2 * count + number // 2].at[pl.ds(number % 2 * rows, rows)]
        copies.append(pltpu.make_async_copy(block, target, arrived.at[number]))
    for copy in copies:
        copy.start()
    for copy in copies:
        copy.wait()


def joined(*pairs):
    blocks = [in_hbm(block) for pair in pairs for block in pair]
    return pl.pallas_call(
        join_kernel,
        in_specs=[pl.BlockSpec(memory_space=pl.ANY)] * len(blocks),
        out_specs=[pl.BlockSpec(memory_space=pltpu.VMEM)] * len(pairs),
        out_shape=[
            jax.ShapeDtypeStruct((2 * first.shape[0], first.shape[1]), first.dtype)
            for first, _ in pairs
        ],
        scratch_shapes=[pltpu.SemaphoreType.DMA((len(blocks),))],
        compiler_params=pltpu.CompilerParams(vmem_limit_bytes=16 * MIB),
        cost_estimate=pl.CostEstimate(
            flops=0,
            bytes_accessed=sum(8 * first.size for first, _ in pairs),
            transcendentals=0,
        ),
        name="join",
    )(*blocks)


def transpose_kernel(n_col, ids, *refs):
    pieces, (out, held) = refs[:n_col], refs[n_col:]
    spread(pieces, ids[1], 1, held)
    out[...] = held[...].T


def transpose(ids, pieces):
    n_col = len(pieces)
    rows, depth = pieces[0].shape
    total = rows // 2 * n_col
    return pl.pallas_call(
        functools.partial(transpose_kernel, n_col),
        grid_spec=pltpu.PrefetchScalarGridSpec(
            num_scalar_prefetch=1,
            grid=(1,),
            in_specs=[whole((rows, depth))] * n_col,
            out_specs=whole((depth, total)),
            scratch_shapes=[pltpu.VMEM((total, depth), BF16)],
        ),
        out_shape=jax.ShapeDtypeStruct((depth, total), BF16),
        compiler_params=pltpu.CompilerParams(vmem_limit_bytes=16 * MIB),
        cost_estimate=pl.CostEstimate(
            flops=0, bytes_accessed=4 * total * depth, transcendentals=0
        ),
        name="inputs_transposed",
    )(ids, *pieces)


def partial_kernel(n_pieces, ids, *refs):
    pieces, weight, refs = refs[:n_pieces], refs[n_pieces], refs[n_pieces + 1 :]
    if n_pieces > 1:
        *outs, tokens = refs

        @pl.when(pl.program_id(0) == 0)
        def _():
            spread(pieces, ids[1], 0, tokens)
    else:
        tokens, outs = pieces[0], refs
    term = contract(tokens[...], weight[...], 1, 1).astype(BF16)
    for number, out in enumerate(outs):

        @pl.when(pl.program_id(0) == number)
        def _():
            out[...] = term


def partials(ids, pieces, weight, first, count):
    rows, depth = pieces[0].shape
    total = rows * len(pieces) // (2 if len(pieces) > 1 else 1)
    units = weight.shape[0] // CHUNKS
    shapes = [(total, units)] * count
    if len(pieces) > 1:
        shapes.append((total, depth))
    return pl.pallas_call(
        functools.partial(partial_kernel, len(pieces)),
        grid_spec=pltpu.PrefetchScalarGridSpec(
            num_scalar_prefetch=1,
            grid=(count,),
            in_specs=[whole((rows, depth))] * len(pieces)
            + [pl.BlockSpec((units, depth), lambda j, *_: (first + j, 0))],
            out_specs=[whole(shape) for shape in shapes],
        ),
        out_shape=[jax.ShapeDtypeStruct(shape, BF16) for shape in shapes],
        compiler_params=pltpu.CompilerParams(vmem_limit_bytes=16 * MIB),
        cost_estimate=pl.CostEstimate(
            flops=2 * total * depth * units * count,
            bytes_accessed=2 * (units * depth * count + total * units * count + total * depth),
            transcendentals=0,
        ),
        name="hidden_grad_partials",
    )(ids, *pieces, in_hbm(weight))


def filled(before):
    before = list(before or [])
    return before, [pl.BlockSpec(memory_space=pl.ANY)] * len(before)


def row_blocks(me, n):
    half = n // 2
    left = me < half
    place = jnp.where(left, me, n - 1 - me)
    near = [lax.rem(place + step, half) for step in range(half)]
    near = [jnp.where(left, at, n - 1 - at) for at in near]
    far = [jnp.where(left, n - 1 - at, at) for at in reversed(range(half))]
    return near + far


def factor_kernel(n, count, ids, *refs):
    sources, outs = refs[:-3], refs[-3:]
    sources = list(sources)
    rows = sources[0].shape[0] // 2
    half = n // 2
    place = jnp.where(ids[0] < half, ids[0], n - 1 - ids[0])
    for number, inner in enumerate(count):
        block = sources.pop(0)[...]
        if inner is not None:
            block = jnp.where(place >= inner[0], block, sources.pop(0)[...])
        gate = block[:rows].astype(F32)
        up = block[rows:].astype(F32)
        sigma = 1.0 / (1.0 + jnp.exp(-gate))
        silu = gate * sigma
        part = pl.ds(number * rows, rows)
        outs[0][part, :] = (up * sigma * (1.0 + gate * (1.0 - sigma))).astype(BF16)
        outs[1][part, :] = silu.astype(BF16)
        outs[2][part, :] = (silu * up).astype(BF16)


def factors_of(ids, sources, n):
    operands, count = [], []
    for source in sources:
        if isinstance(source, tuple):
            inner, block, other = source
            operands += [block, other]
            count.append((inner,))
        else:
            operands.append(source)
            count.append(None)
    rows, width = operands[0].shape
    rows = rows // 2 * len(sources)
    tile = tile_of(width, 512)
    out = pl.BlockSpec((rows, tile), lambda j, *_: (0, j))
    return pl.pallas_call(
        functools.partial(factor_kernel, n, count),
        grid_spec=pltpu.PrefetchScalarGridSpec(
            num_scalar_prefetch=1,
            grid=(width // tile,),
            in_specs=[pl.BlockSpec((operands[0].shape[0], tile), lambda j, *_: (0, j))]
            * len(operands),
            out_specs=[out] * 3,
        ),
        out_shape=[jax.ShapeDtypeStruct((rows, width), BF16)] * 3,
        compiler_params=pltpu.CompilerParams(vmem_limit_bytes=16 * MIB),
        cost_estimate=pl.CostEstimate(
            flops=10 * rows * width,
            bytes_accessed=4 * rows * width + 6 * rows * width,
            transcendentals=rows * width,
        ),
        name="factors",
    )(ids, *operands)


def down_kernel(n, ids, early, late, cotangent, out, hidden):
    rows = late.shape[0]
    for number, block in enumerate(row_blocks(ids[0], n)):
        source = late if number == n - 1 else early
        part = pl.ds(0 if number == n - 1 else number * rows, rows)
        hidden[rows_at(block * rows, rows), :] = source[part, :]
    out[...] = contract(hidden[...], cotangent[...], 0, 0).astype(BF16)


def down_grads(ids, early, late, cotangent, n):
    total, depth = cotangent.shape
    width = late.shape[1]
    tile = tile_of(width, 512)
    return pl.pallas_call(
        functools.partial(down_kernel, n),
        grid_spec=pltpu.PrefetchScalarGridSpec(
            num_scalar_prefetch=1,
            grid=(width // tile,),
            in_specs=[
                pl.BlockSpec((early.shape[0], tile), lambda j, *_: (0, j)),
                pl.BlockSpec((late.shape[0], tile), lambda j, *_: (0, j)),
                whole((total, depth)),
            ],
            out_specs=pl.BlockSpec((tile, depth), lambda j, *_: (j, 0)),
            scratch_shapes=[pltpu.VMEM((total, tile), BF16)],
        ),
        out_shape=jax.ShapeDtypeStruct((width, depth), BF16),
        compiler_params=pltpu.CompilerParams(vmem_limit_bytes=20 * MIB),
        cost_estimate=pl.CostEstimate(
            flops=2 * total * depth * width,
            bytes_accessed=2 * (width * depth + total * depth + total * width),
            transcendentals=0,
        ),
        name="down_grad",
    )(ids, early, late, cotangent)


def delta_kernel(n, n_col, first, last, ids, *refs):
    middle, got, *factors, gate_weight, up_weight = refs[:8]
    refs = list(refs[8:])
    before = None if first else refs.pop(0)
    gate_out, up_out = refs[:2]

    @pl.when(pl.program_id(0) == 0)
    def _():
        outer = jnp.logical_or(ids[0] == 0, ids[0] == n - 1)
        rows = middle.shape[0] // n
        for number, block in enumerate(row_blocks(ids[0], n)):
            part = rows_at(block * rows, rows)
            grad = jnp.where(outer, got[part, :], middle[part, :]).astype(F32)
            late = number == n - 1
            source = pl.ds(0 if late else number * rows, rows)
            gate_factor, up_factor = factors[2:] if late else factors[:2]
            gate_out[part, :] = (grad * gate_factor[source, :].astype(F32)).astype(BF16)
            up_out[part, :] = (grad * up_factor[source, :].astype(F32)).astype(BF16)

    term = contract(gate_out[...], gate_weight[...], 1, 1) + contract(
        up_out[...], up_weight[...], 1, 1
    )
    if not first:
        term += before[...]
    if not last:
        refs[2][...] = term
        return
    keep, send, result = refs[2:]
    result[...] = term
    rows = keep.shape[1]
    for slot in range(n_col):
        out = send if slot % 2 else keep
        start = jnp.bitwise_xor(ids[1], slot) * rows
        out[slot // 2] = result[rows_at(start, rows), :].astype(BF16)


def deltas(ids, grads, factors, weights, n, n_col, chunk, before):
    total, units = grads[0].shape
    depth = weights[0].shape[0]
    rows = total // n_col
    tile = tile_of(depth, 512)
    tall = whole((total, units))
    wide = pl.BlockSpec((tile, units), lambda j, *_: (j, chunk))
    running = pl.BlockSpec((total, tile), lambda j, *_: (0, j))
    delta_shape = jax.ShapeDtypeStruct((total, units), BF16)
    last = chunk == CHUNKS - 1
    if last:
        half = pl.BlockSpec((n_col // 2, rows, tile), lambda j, *_: (0, 0, j))
        out_specs = [half, half]
        out_shape = [jax.ShapeDtypeStruct((n_col // 2, rows, depth), BF16)] * 2
        scratch = [pltpu.VMEM((total, tile), F32)]
    else:
        out_specs, scratch = [running], []
        out_shape = [jax.ShapeDtypeStruct((total, depth), F32)]
    more = [] if before is None else [before]
    factor_specs = [
        pl.BlockSpec((factor.shape[0], units), lambda j, *_: (0, chunk)) for factor in factors
    ]
    return pl.pallas_call(
        functools.partial(delta_kernel, n, n_col, before is None, last),
        grid_spec=pltpu.PrefetchScalarGridSpec(
            num_scalar_prefetch=1,
            grid=(depth // tile,),
            in_specs=[tall] * 2 + factor_specs + [wide] * 2 + [running] * len(more),
            out_specs=[tall, tall] + out_specs,
            scratch_shapes=scratch,
        ),
        out_shape=[delta_shape, delta_shape] + out_shape,
        compiler_params=pltpu.CompilerParams(vmem_limit_bytes=28 * MIB),
        cost_estimate=NO_COST,
        name="deltas_and_input_grad",
    )(ids, *grads, *factors, *weights, *more)


def weight_grad_kernel(inputs, gate_delta, up_delta, *refs):
    gate_out, up_out = refs[-2:]
    gate_out[...] = contract(inputs[...], gate_delta[...], 1, 0).astype(BF16)
    up_out[...] = contract(inputs[...], up_delta[...], 1, 0).astype(BF16)


def weight_grads(inputs_t, gate_delta, up_delta, chunk, before):
    depth, total = inputs_t.shape
    units = gate_delta.shape[1]
    tile = tile_of(depth, 512)
    more, more_specs = filled(before)
    out = pl.BlockSpec((tile, units), lambda j: (j, chunk))
    cost = NO_COST
    if chunk == CHUNKS - 1:
        cost = pl.CostEstimate(
            flops=4 * total * depth * units,
            bytes_accessed=4 * units * depth + 4 * total * units + 2 * total * depth,
            transcendentals=0,
        )
    return pl.pallas_call(
        weight_grad_kernel,
        grid=(depth // tile,),
        in_specs=[pl.BlockSpec((tile, total), lambda j: (j, 0))]
        + [whole((total, units))] * 2
        + more_specs,
        out_specs=[out, out],
        out_shape=[jax.ShapeDtypeStruct((depth, units * CHUNKS), BF16)] * 2,
        input_output_aliases={3: 0, 4: 1} if more else {},
        compiler_params=pltpu.CompilerParams(vmem_limit_bytes=16 * MIB),
        cost_estimate=cost,
        name="gate_and_up_grad",
    )(inputs_t, gate_delta, up_delta, *more)


def add(left, right):
    return (left.astype(F32) + right.astype(F32)).astype(BF16)


def on_device(
    n_row, n_col, inputs, cotangent, gate_pre, up_pre, gate_weight, up_weight, down_weight
):
    me = lax.axis_index("row")
    ids = jnp.stack([me, lax.axis_index("col")]).astype(jnp.int32)
    half = n_row // 2
    place = jnp.where(me < half, me, n_row - 1 - me)

    pre, token_block = joined((gate_pre, up_pre), (cotangent, inputs))
    ins, outs = own_half(pre, n_row)
    sources = [pre]
    for step in range(1, half):
        sources.append(outs[step] if half == 2 else (half - step, ins[half - step], outs[step]))
    far = [lax.ppermute(block, "row", across(n_row)) for block in ins]
    away = [sent_out(block, place, n_row) for block in far]
    sources += [(1, *pair) for pair in away]

    pieces = cube_gather(token_block, n_col)
    term, tokens = partials(ids, pieces, down_weight, 0, 1)
    tokens = after(tokens, ins[-1], far[0])
    terms = [term, *partials(ids, [tokens], down_weight, 1, CHUNKS - 1)]
    inputs_t = transpose(ids, pieces)

    early = factors_of(ids, sources[:-1], n_row)
    late = factors_of(ids, sources[-1:], n_row)
    factors = [*early[:2], *late[:2]]
    before = {0: early, 2: late}
    running = weight_out = met = None
    sent = []

    def work_on(chunk, running, weight_out):
        gate_delta, up_delta, *running = deltas(
            ids,
            sent[chunk],
            factors,
            (gate_weight, up_weight),
            n_row,
            n_col,
            chunk,
            running,
        )
        weight_out = weight_grads(inputs_t, gate_delta, up_delta, chunk, weight_out)
        if chunk == CHUNKS - 1:
            return running, weight_out
        running, *weight_out = lax.optimization_barrier((running[0], *weight_out))
        return running, weight_out

    for chunk, held in enumerate(terms):
        for step in range(half - 1):
            if met is not None:
                held = after(held, met)
            got = met = lax.ppermute(held, "row", inward([step], n_row))
            if chunk == 0:
                got = after(got, terms[-1], far[-1], away[0][1], inputs_t)
            held = add(held, got)
        got = lax.ppermute(held, "row", across(n_row))
        if chunk == CHUNKS - 1:
            sent[0] = (sent[0][0], after(sent[0][1], sent[2][0]))
            running, weight_out = work_on(0, None, None)
            got, running, *weight_out = lax.optimization_barrier((got, running, *weight_out))
        elif chunk in before:
            got = after(got, *before[chunk])
        held = add(held, got)
        if chunk == 1:
            held = after(held, away[-1][1])
        sent.append(sent_out(held, place, n_row))

    for chunk in range(1, CHUNKS):
        if chunk == CHUNKS - 2:
            hidden = after(late[2], running)
            down_grad = down_grads(ids, early[2], hidden, tokens, n_row)
            running, down_grad = lax.optimization_barrier((running, down_grad))
        running, weight_out = work_on(chunk, running, weight_out)
    gate_grad, up_grad = weight_out
    keep, send = running

    keep = add(keep, lax.ppermute(send, "col", [(i, i ^ 1) for i in range(n_col)]))
    input_grad = keep[0].astype(F32)
    for number in range(1, n_col // 2):
        pairs = [(i, i ^ (2 * number)) for i in range(n_col)]
        input_grad += lax.ppermute(keep[number], "col", pairs).astype(F32)
    input_grad = input_grad.astype(BF16)
    return (input_grad, gate_grad, up_grad, down_grad)


def solution(mesh):
    placed = (
        P("col", "row"),
        P("col", "row"),
        P("row", "col"),
        P("row", "col"),
        P("row", "col"),
        P("row", "col"),
        P("col", "row"),
    )
    return jax.shard_map(
        functools.partial(on_device, mesh.shape["row"], mesh.shape["col"]),
        mesh=mesh,
        in_specs=placed,
        out_specs=(P("col", "row"), P("row", "col"), P("row", "col"), P("col", "row")),
        check_vma=False,
    )
```

```python
import functools

import jax
import jax.numpy as jnp
from jax import lax
from jax.experimental import pallas as pl
from jax.experimental.pallas import tpu as pltpu
from jax.sharding import PartitionSpec as P

F32 = jnp.float32
BF16 = jnp.bfloat16
MIB = 1024 * 1024
NO_COST = pl.CostEstimate(flops=0, bytes_accessed=0, transcendentals=0)
CHUNKS = 4


def contract(left, right, left_dim, right_dim):
    return lax.dot_general(
        left, right, (((left_dim,), (right_dim,)), ((), ())), preferred_element_type=F32
    )


def whole(shape):
    return pl.BlockSpec(shape, lambda *_: (0,) * len(shape))


def tile_of(size, most):
    tile = min(size, most)
    while size % tile:
        tile //= 2
    return tile


def after(value, *others):
    return lax.optimization_barrier((value, *others))[0]


def inward(places, n):
    return [pair for p in places for pair in ((p, p + 1), (n - 1 - p, n - 2 - p))]


def outward(places, n):
    return [(target, source) for source, target in inward(places, n)]


def across(n):
    return [(n // 2 - 1, n // 2), (n // 2, n // 2 - 1)]


def own_half(block, n):
    half = n // 2
    ins, outs = [block], [block]
    for step in range(1, half):
        if half == 2:
            met = lax.ppermute(block, "row", inward([0], n) + outward([0], n))
            ins.append(met)
            outs.append(met)
        else:
            ins.append(lax.ppermute(ins[-1], "row", inward(range(step - 1, half - 1), n)))
            outs.append(lax.ppermute(outs[-1], "row", outward(range(half - step), n)))
    return ins, outs


def sent_out(block, place, n):
    got = block
    for step in reversed(range(n // 2 - 1)):
        if step < n // 2 - 2:
            block = jnp.where(place == step + 1, got, block)
        got = lax.ppermute(block, "row", outward([step], n))
    return block, got


def cube_bits(n):
    bits, bit = [], 1
    while bit < n:
        bits.append(bit)
        bit *= 2
    return bits


def cube_gather(block, n):
    pieces = {0: block}
    for bit in reversed(cube_bits(n)):
        pairs = [(i, i ^ bit) for i in range(n)]
        for slot in list(pieces):
            pieces[slot | bit] = lax.ppermute(pieces[slot], "col", pairs)
    return [pieces[k] for k in range(n)]


def rows_at(start, rows):
    return pl.ds(pl.multiple_of(start, 16), rows)


def spread(pieces, col, which, target):
    for slot, piece in enumerate(pieces):
        rows = piece.shape[0] // 2
        block = piece[which * rows : (which + 1) * rows, :]
        target[rows_at(jnp.bitwise_xor(col, slot) * rows, rows), :] = block


def in_hbm(array):
    return pltpu.with_memory_space_constraint(array, pltpu.HBM)


def join_kernel(*refs):
    arrived = refs[-1]
    count = len(refs) // 3
    copies = []
    for number, block in enumerate(refs[: 2 * count]):
        rows = block.shape[0]
        target = refs[2 * count + number // 2].at[pl.ds(number % 2 * rows, rows)]
        copies.append(pltpu.make_async_copy(block, target, arrived.at[number]))
    for copy in copies:
        copy.start()
    for copy in copies:
        copy.wait()


def joined(*pairs):
    blocks = [in_hbm(block) for pair in pairs for block in pair]
    return pl.pallas_call(
        join_kernel,
        in_specs=[pl.BlockSpec(memory_space=pl.ANY)] * len(blocks),
        out_specs=[pl.BlockSpec(memory_space=pltpu.VMEM)] * len(pairs),
        out_shape=[
            jax.ShapeDtypeStruct((2 * first.shape[0], first.shape[1]), first.dtype)
            for first, _ in pairs
        ],
        scratch_shapes=[pltpu.SemaphoreType.DMA((len(blocks),))],
        compiler_params=pltpu.CompilerParams(vmem_limit_bytes=16 * MIB),
        cost_estimate=pl.CostEstimate(
            flops=0,
            bytes_accessed=sum(8 * first.size for first, _ in pairs),
            transcendentals=0,
        ),
        name="join",
    )(*blocks)


def transpose_kernel(n_col, ids, *refs):
    pieces, (out, held) = refs[:n_col], refs[n_col:]
    spread(pieces, ids[1], 1, held)
    out[...] = held[...].T


def transpose(ids, pieces):
    n_col = len(pieces)
    rows, depth = pieces[0].shape
    total = rows // 2 * n_col
    return pl.pallas_call(
        functools.partial(transpose_kernel, n_col),
        grid_spec=pltpu.PrefetchScalarGridSpec(
            num_scalar_prefetch=1,
            grid=(1,),
            in_specs=[whole((rows, depth))] * n_col,
            out_specs=whole((depth, total)),
            scratch_shapes=[pltpu.VMEM((total, depth), BF16)],
        ),
        out_shape=jax.ShapeDtypeStruct((depth, total), BF16),
        compiler_params=pltpu.CompilerParams(vmem_limit_bytes=16 * MIB),
        cost_estimate=pl.CostEstimate(
            flops=0, bytes_accessed=4 * total * depth, transcendentals=0
        ),
        name="inputs_transposed",
    )(ids, *pieces)


def partial_kernel(n_pieces, ids, *refs):
    pieces, weight, refs = refs[:n_pieces], refs[n_pieces], refs[n_pieces + 1 :]
    if n_pieces > 1:
        *outs, tokens = refs

        @pl.when(pl.program_id(0) == 0)
        def _():
            spread(pieces, ids[1], 0, tokens)
    else:
        tokens, outs = pieces[0], refs
    term = contract(tokens[...], weight[...], 1, 1).astype(BF16)
    for number, out in enumerate(outs):

        @pl.when(pl.program_id(0) == number)
        def _():
            out[...] = term


def partials(ids, pieces, weight, first, count):
    rows, depth = pieces[0].shape
    total = rows * len(pieces) // (2 if len(pieces) > 1 else 1)
    units = weight.shape[0] // CHUNKS
    shapes = [(total, units)] * count
    if len(pieces) > 1:
        shapes.append((total, depth))
    return pl.pallas_call(
        functools.partial(partial_kernel, len(pieces)),
        grid_spec=pltpu.PrefetchScalarGridSpec(
            num_scalar_prefetch=1,
            grid=(count,),
            in_specs=[whole((rows, depth))] * len(pieces)
            + [pl.BlockSpec((units, depth), lambda j, *_: (first + j, 0))],
            out_specs=[whole(shape) for shape in shapes],
        ),
        out_shape=[jax.ShapeDtypeStruct(shape, BF16) for shape in shapes],
        compiler_params=pltpu.CompilerParams(vmem_limit_bytes=16 * MIB),
        cost_estimate=pl.CostEstimate(
            flops=2 * total * depth * units * count,
            bytes_accessed=2 * (units * depth * count + total * units * count + total * depth),
            transcendentals=0,
        ),
        name="hidden_grad_partials",
    )(ids, *pieces, in_hbm(weight))


def filled(before):
    before = list(before or [])
    return before, [pl.BlockSpec(memory_space=pl.ANY)] * len(before)


def row_blocks(me, n):
    half = n // 2
    left = me < half
    place = jnp.where(left, me, n - 1 - me)
    near = [lax.rem(place + step, half) for step in range(half)]
    near = [jnp.where(left, at, n - 1 - at) for at in near]
    far = [jnp.where(left, n - 1 - at, at) for at in reversed(range(half))]
    return near + far


def factor_kernel(n, count, ids, *refs):
    sources, outs = refs[:-3], refs[-3:]
    sources = list(sources)
    rows = sources[0].shape[0] // 2
    half = n // 2
    place = jnp.where(ids[0] < half, ids[0], n - 1 - ids[0])
    for number, inner in enumerate(count):
        block = sources.pop(0)[...]
        if inner is not None:
            block = jnp.where(place >= inner[0], block, sources.pop(0)[...])
        gate = block[:rows].astype(F32)
        up = block[rows:].astype(F32)
        sigma = 1.0 / (1.0 + jnp.exp(-gate))
        silu = gate * sigma
        part = pl.ds(number * rows, rows)
        outs[0][part, :] = (up * sigma * (1.0 + gate * (1.0 - sigma))).astype(BF16)
        outs[1][part, :] = silu.astype(BF16)
        outs[2][part, :] = (silu * up).astype(BF16)


def factors_of(ids, sources, n):
    operands, count = [], []
    for source in sources:
        if isinstance(source, tuple):
            inner, block, other = source
            operands += [block, other]
            count.append((inner,))
        else:
            operands.append(source)
            count.append(None)
    rows, width = operands[0].shape
    rows = rows // 2 * len(sources)
    tile = tile_of(width, 512)
    out = pl.BlockSpec((rows, tile), lambda j, *_: (0, j))
    return pl.pallas_call(
        functools.partial(factor_kernel, n, count),
        grid_spec=pltpu.PrefetchScalarGridSpec(
            num_scalar_prefetch=1,
            grid=(width // tile,),
            in_specs=[pl.BlockSpec((operands[0].shape[0], tile), lambda j, *_: (0, j))]
            * len(operands),
            out_specs=[out] * 3,
        ),
        out_shape=[jax.ShapeDtypeStruct((rows, width), BF16)] * 3,
        compiler_params=pltpu.CompilerParams(vmem_limit_bytes=16 * MIB),
        cost_estimate=pl.CostEstimate(
            flops=10 * rows * width,
            bytes_accessed=10 * rows * width * (8 if len(sources) == 1 else 1),
            transcendentals=rows * width,
        ),
        name="factors",
    )(ids, *operands)


def down_kernel(n, ids, early, late, cotangent, out, hidden):
    rows = late.shape[0]
    for number, block in enumerate(row_blocks(ids[0], n)):
        source = late if number == n - 1 else early
        part = pl.ds(0 if number == n - 1 else number * rows, rows)
        hidden[rows_at(block * rows, rows), :] = source[part, :]
    out[...] = contract(hidden[...], cotangent[...], 0, 0).astype(BF16)


def down_grads(ids, early, late, cotangent, n):
    total, depth = cotangent.shape
    width = late.shape[1]
    tile = tile_of(width, 512)
    return pl.pallas_call(
        functools.partial(down_kernel, n),
        grid_spec=pltpu.PrefetchScalarGridSpec(
            num_scalar_prefetch=1,
            grid=(width // tile,),
            in_specs=[
                pl.BlockSpec((early.shape[0], tile), lambda j, *_: (0, j)),
                pl.BlockSpec((late.shape[0], tile), lambda j, *_: (0, j)),
                whole((total, depth)),
            ],
            out_specs=pl.BlockSpec((tile, depth), lambda j, *_: (j, 0)),
            scratch_shapes=[pltpu.VMEM((total, tile), BF16)],
        ),
        out_shape=jax.ShapeDtypeStruct((width, depth), BF16),
        compiler_params=pltpu.CompilerParams(vmem_limit_bytes=20 * MIB),
        cost_estimate=pl.CostEstimate(
            flops=2 * total * depth * width,
            bytes_accessed=2 * (width * depth + total * depth + total * width),
            transcendentals=0,
        ),
        name="down_grad",
    )(ids, early, late, cotangent)


def delta_kernel(n, n_col, first, last, ids, *refs):
    middle, got, *factors, gate_weight, up_weight = refs[:8]
    refs = list(refs[8:])
    before = None if first else refs.pop(0)
    if last:
        gate_out, up_out = refs[:2]
    else:
        inputs = refs.pop(0)
        running, gate_grad, up_grad, gate_out, up_out = refs[-5:]

    @pl.when(pl.program_id(0) == 0)
    def _():
        outer = jnp.logical_or(ids[0] == 0, ids[0] == n - 1)
        rows = middle.shape[0] // n
        for number, block in enumerate(row_blocks(ids[0], n)):
            part = rows_at(block * rows, rows)
            grad = jnp.where(outer, got[part, :], middle[part, :]).astype(F32)
            late = number == n - 1
            source = pl.ds(0 if late else number * rows, rows)
            gate_factor, up_factor = factors[2:] if late else factors[:2]
            gate_out[part, :] = (grad * gate_factor[source, :].astype(F32)).astype(BF16)
            up_out[part, :] = (grad * up_factor[source, :].astype(F32)).astype(BF16)

    term = contract(gate_out[...], gate_weight[...], 1, 1) + contract(
        up_out[...], up_weight[...], 1, 1
    )
    if not first:
        term += before[...]
    if not last:
        running[...] = term
        gate_grad[...] = contract(inputs[...], gate_out[...], 1, 0).astype(BF16)
        up_grad[...] = contract(inputs[...], up_out[...], 1, 0).astype(BF16)
        return
    keep, send, result = refs[2:]
    result[...] = term
    rows = keep.shape[1]
    for slot in range(n_col):
        out = send if slot % 2 else keep
        start = jnp.bitwise_xor(ids[1], slot) * rows
        out[slot // 2] = result[rows_at(start, rows), :].astype(BF16)


def deltas(ids, grads, factors, weights, inputs_t, n, n_col, chunk, before, weight_out):
    total, units = grads[0].shape
    depth, width = weights[0].shape
    rows = total // n_col
    tile = tile_of(depth, 512)
    tall = whole((total, units))
    wide = pl.BlockSpec((tile, units), lambda j, *_: (j, chunk))
    running = pl.BlockSpec((total, tile), lambda j, *_: (0, j))
    delta_shape = (total, units)
    last = chunk == CHUNKS - 1
    more = [] if before is None else [before]
    more_specs = [running] * len(more)
    aliases = {}
    if last:
        half = pl.BlockSpec((n_col // 2, rows, tile), lambda j, *_: (0, 0, j))
        out_specs = [tall, tall, half, half]
        out_shape = [jax.ShapeDtypeStruct(delta_shape, BF16)] * 2
        out_shape += [jax.ShapeDtypeStruct((n_col // 2, rows, depth), BF16)] * 2
        scratch = [pltpu.VMEM((total, tile), F32)]
    else:
        more.append(inputs_t)
        more_specs.append(pl.BlockSpec((tile, total), lambda j, *_: (j, 0)))
        held, held_specs = filled(weight_out)
        aliases = {9 + len(more) + number: 1 + number for number in range(len(held))}
        more += held
        more_specs += held_specs
        out_specs = [running, wide, wide]
        out_shape = [jax.ShapeDtypeStruct((total, depth), F32)]
        out_shape += [jax.ShapeDtypeStruct((depth, width), BF16)] * 2
        scratch = [pltpu.VMEM(delta_shape, BF16)] * 2
    factor_specs = [
        pl.BlockSpec((factor.shape[0], units), lambda j, *_: (0, chunk)) for factor in factors
    ]
    return pl.pallas_call(
        functools.partial(delta_kernel, n, n_col, before is None, last),
        grid_spec=pltpu.PrefetchScalarGridSpec(
            num_scalar_prefetch=1,
            grid=(depth // tile,),
            in_specs=[tall] * 2 + factor_specs + [wide] * 2 + more_specs,
            out_specs=out_specs,
            scratch_shapes=scratch,
        ),
        out_shape=out_shape,
        input_output_aliases=aliases,
        compiler_params=pltpu.CompilerParams(vmem_limit_bytes=28 * MIB),
        cost_estimate=NO_COST,
        name="chunk",
    )(ids, *grads, *factors, *weights, *more)


def weight_grad_kernel(inputs, gate_delta, up_delta, *refs):
    gate_out, up_out = refs[-2:]
    gate_out[...] = contract(inputs[...], gate_delta[...], 1, 0).astype(BF16)
    up_out[...] = contract(inputs[...], up_delta[...], 1, 0).astype(BF16)


def weight_grads(inputs_t, gate_delta, up_delta, chunk, before):
    depth, total = inputs_t.shape
    units = gate_delta.shape[1]
    tile = tile_of(depth, 512)
    more, more_specs = filled(before)
    out = pl.BlockSpec((tile, units), lambda j: (j, chunk))
    cost = NO_COST
    if chunk == CHUNKS - 1:
        cost = pl.CostEstimate(
            flops=4 * total * depth * units,
            bytes_accessed=4 * units * depth + 4 * total * units + 2 * total * depth,
            transcendentals=0,
        )
    return pl.pallas_call(
        weight_grad_kernel,
        grid=(depth // tile,),
        in_specs=[pl.BlockSpec((tile, total), lambda j: (j, 0))]
        + [whole((total, units))] * 2
        + more_specs,
        out_specs=[out, out],
        out_shape=[jax.ShapeDtypeStruct((depth, units * CHUNKS), BF16)] * 2,
        input_output_aliases={3: 0, 4: 1} if more else {},
        compiler_params=pltpu.CompilerParams(vmem_limit_bytes=16 * MIB),
        cost_estimate=cost,
        name="gate_and_up_grad",
    )(inputs_t, gate_delta, up_delta, *more)


def add(left, right):
    return (left.astype(F32) + right.astype(F32)).astype(BF16)


def on_device(
    n_row, n_col, inputs, cotangent, gate_pre, up_pre, gate_weight, up_weight, down_weight
):
    me = lax.axis_index("row")
    ids = jnp.stack([me, lax.axis_index("col")]).astype(jnp.int32)
    half = n_row // 2
    place = jnp.where(me < half, me, n_row - 1 - me)

    pre, token_block = joined((gate_pre, up_pre), (cotangent, inputs))
    ins, outs = own_half(pre, n_row)
    sources = [pre]
    for step in range(1, half):
        sources.append(outs[step] if half == 2 else (half - step, ins[half - step], outs[step]))
    far = [lax.ppermute(block, "row", across(n_row)) for block in ins]
    away = [sent_out(block, place, n_row) for block in far]
    sources += [(1, *pair) for pair in away]

    pieces = cube_gather(token_block, n_col)
    term, tokens = partials(ids, pieces, down_weight, 0, 1)
    tokens = after(tokens, ins[-1], far[0])
    terms = [term, *partials(ids, [tokens], down_weight, 1, CHUNKS - 1)]
    inputs_t = transpose(ids, pieces)

    early = factors_of(ids, sources[:-1], n_row)
    late = factors_of(ids, sources[-1:], n_row)
    factors = [*early[:2], *late[:2]]
    before = {0: [*early, *late]}
    running = weight_out = met = None
    sent = []

    def work_on(chunk, running, weight_out):
        made = deltas(
            ids,
            sent[chunk],
            factors,
            (gate_weight, up_weight),
            inputs_t,
            n_row,
            n_col,
            chunk,
            running,
            weight_out,
        )
        if chunk < CHUNKS - 1:
            running, *weight_out = lax.optimization_barrier(tuple(made))
            return running, weight_out
        gate_delta, up_delta, *running = made
        return running, weight_grads(inputs_t, gate_delta, up_delta, chunk, weight_out)

    for chunk, held in enumerate(terms):
        for step in range(half - 1):
            if met is not None:
                held = after(held, met)
            got = lax.ppermute(held, "row", inward([step], n_row))
            met = got
            if chunk == 0:
                got = after(got, terms[-1], far[-1], away[0][1], inputs_t)
            held = add(held, got)
        if chunk == 1:
            held = after(held, crossed)
        got = crossed = lax.ppermute(held, "row", across(n_row))
        if chunk == CHUNKS - 1:
            sent[0] = (sent[0][0], after(sent[0][1], sent[2][0]))
            running, weight_out = work_on(0, None, None)
            got, running, *weight_out = lax.optimization_barrier((got, running, *weight_out))
        elif chunk in before:
            got = after(got, *before[chunk])
        held = add(held, got)
        sent.append(sent_out(held, place, n_row))

    for chunk in range(1, CHUNKS):
        running, weight_out = work_on(chunk, running, weight_out)
    gate_grad, up_grad = weight_out
    keep, send = running
    down_grad = down_grads(ids, early[2], after(late[2], send), tokens, n_row)

    keep = add(keep, lax.ppermute(send, "col", [(i, i ^ 1) for i in range(n_col)]))
    input_grad = keep[0].astype(F32)
    for number in range(1, n_col // 2):
        pairs = [(i, i ^ (2 * number)) for i in range(n_col)]
        input_grad += lax.ppermute(keep[number], "col", pairs).astype(F32)
    input_grad = input_grad.astype(BF16)
    return (input_grad, gate_grad, up_grad, down_grad)


def solution(mesh):
    placed = (
        P("col", "row"),
        P("col", "row"),
        P("row", "col"),
        P("row", "col"),
        P("row", "col"),
        P("row", "col"),
        P("col", "row"),
    )
    return jax.shard_map(
        functools.partial(on_device, mesh.shape["row"], mesh.shape["col"]),
        mesh=mesh,
        in_specs=placed,
        out_specs=(P("col", "row"), P("row", "col"), P("row", "col"), P("col", "row")),
        check_vma=False,
    )
```

```python
import functools

import jax
import jax.numpy as jnp
from jax import lax
from jax.experimental import pallas as pl
from jax.experimental.pallas import tpu as pltpu
from jax.sharding import PartitionSpec as P

F32 = jnp.float32
BF16 = jnp.bfloat16
MIB = 1024 * 1024
NO_COST = pl.CostEstimate(flops=0, bytes_accessed=0, transcendentals=0)
CHUNKS = 4


def contract(left, right, left_dim, right_dim):
    return lax.dot_general(
        left, right, (((left_dim,), (right_dim,)), ((), ())), preferred_element_type=F32
    )


def whole(shape):
    return pl.BlockSpec(shape, lambda *_: (0,) * len(shape))


def tile_of(size, most):
    tile = min(size, most)
    while size % tile:
        tile //= 2
    return tile


def after(value, *others):
    return lax.optimization_barrier((value, *others))[0]


def inward(places, n):
    return [pair for p in places for pair in ((p, p + 1), (n - 1 - p, n - 2 - p))]


def outward(places, n):
    return [(target, source) for source, target in inward(places, n)]


def across(n):
    return [(n // 2 - 1, n // 2), (n // 2, n // 2 - 1)]


def own_half(block, n):
    half = n // 2
    ins, outs = [block], [block]
    for step in range(1, half):
        if half == 2:
            met = lax.ppermute(block, "row", inward([0], n) + outward([0], n))
            ins.append(met)
            outs.append(met)
        else:
            ins.append(lax.ppermute(ins[-1], "row", inward(range(step - 1, half - 1), n)))
            outs.append(lax.ppermute(outs[-1], "row", outward(range(half - step), n)))
    return ins, outs


def sent_out(block, place, n):
    got = block
    for step in reversed(range(n // 2 - 1)):
        if step < n // 2 - 2:
            block = jnp.where(place == step + 1, got, block)
        got = lax.ppermute(block, "row", outward([step], n))
    return block, got


def cube_bits(n):
    bits, bit = [], 1
    while bit < n:
        bits.append(bit)
        bit *= 2
    return bits


def cube_gather(block, n):
    pieces = {0: block}
    for bit in reversed(cube_bits(n)):
        pairs = [(i, i ^ bit) for i in range(n)]
        for slot in list(pieces):
            pieces[slot | bit] = lax.ppermute(pieces[slot], "col", pairs)
    return [pieces[k] for k in range(n)]


def rows_at(start, rows):
    return pl.ds(pl.multiple_of(start, 16), rows)


def spread(pieces, col, which, target):
    for slot, piece in enumerate(pieces):
        rows = piece.shape[0] // 2
        block = piece[which * rows : (which + 1) * rows, :]
        target[rows_at(jnp.bitwise_xor(col, slot) * rows, rows), :] = block


def in_hbm(array):
    return pltpu.with_memory_space_constraint(array, pltpu.HBM)


def join_kernel(*refs):
    arrived = refs[-1]
    count = len(refs) // 3
    copies = []
    for number, block in enumerate(refs[: 2 * count]):
        rows = block.shape[0]
        target = refs[2 * count + number // 2].at[pl.ds(number % 2 * rows, rows)]
        copies.append(pltpu.make_async_copy(block, target, arrived.at[number]))
    for copy in copies:
        copy.start()
    for copy in copies:
        copy.wait()


def joined(*pairs):
    blocks = [in_hbm(block) for pair in pairs for block in pair]
    return pl.pallas_call(
        join_kernel,
        in_specs=[pl.BlockSpec(memory_space=pl.ANY)] * len(blocks),
        out_specs=[pl.BlockSpec(memory_space=pltpu.VMEM)] * len(pairs),
        out_shape=[
            jax.ShapeDtypeStruct((2 * first.shape[0], first.shape[1]), first.dtype)
            for first, _ in pairs
        ],
        scratch_shapes=[pltpu.SemaphoreType.DMA((len(blocks),))],
        compiler_params=pltpu.CompilerParams(vmem_limit_bytes=16 * MIB),
        cost_estimate=pl.CostEstimate(
            flops=0,
            bytes_accessed=sum(8 * first.size for first, _ in pairs),
            transcendentals=0,
        ),
        name="join",
    )(*blocks)


def transpose_kernel(n_col, ids, *refs):
    pieces, (out, held) = refs[:n_col], refs[n_col:]
    spread(pieces, ids[1], 1, held)
    out[...] = held[...].T


def transpose(ids, pieces):
    n_col = len(pieces)
    rows, depth = pieces[0].shape
    total = rows // 2 * n_col
    return pl.pallas_call(
        functools.partial(transpose_kernel, n_col),
        grid_spec=pltpu.PrefetchScalarGridSpec(
            num_scalar_prefetch=1,
            grid=(1,),
            in_specs=[whole((rows, depth))] * n_col,
            out_specs=whole((depth, total)),
            scratch_shapes=[pltpu.VMEM((total, depth), BF16)],
        ),
        out_shape=jax.ShapeDtypeStruct((depth, total), BF16),
        compiler_params=pltpu.CompilerParams(vmem_limit_bytes=16 * MIB),
        cost_estimate=pl.CostEstimate(
            flops=0, bytes_accessed=4 * total * depth, transcendentals=0
        ),
        name="inputs_transposed",
    )(ids, *pieces)


def partial_kernel(n_pieces, ids, *refs):
    pieces, weight, refs = refs[:n_pieces], refs[n_pieces], refs[n_pieces + 1 :]
    if n_pieces > 1:
        *outs, tokens = refs

        @pl.when(pl.program_id(0) == 0)
        def _():
            spread(pieces, ids[1], 0, tokens)
    else:
        tokens, outs = pieces[0], refs
    term = contract(tokens[...], weight[...], 1, 1).astype(BF16)
    for number, out in enumerate(outs):

        @pl.when(pl.program_id(0) == number)
        def _():
            out[...] = term


def partials(ids, pieces, weight, first, count):
    rows, depth = pieces[0].shape
    total = rows * len(pieces) // (2 if len(pieces) > 1 else 1)
    units = weight.shape[0] // CHUNKS
    shapes = [(total, units)] * count
    if len(pieces) > 1:
        shapes.append((total, depth))
    return pl.pallas_call(
        functools.partial(partial_kernel, len(pieces)),
        grid_spec=pltpu.PrefetchScalarGridSpec(
            num_scalar_prefetch=1,
            grid=(count,),
            in_specs=[whole((rows, depth))] * len(pieces)
            + [pl.BlockSpec((units, depth), lambda j, *_: (first + j, 0))],
            out_specs=[whole(shape) for shape in shapes],
        ),
        out_shape=[jax.ShapeDtypeStruct(shape, BF16) for shape in shapes],
        compiler_params=pltpu.CompilerParams(vmem_limit_bytes=16 * MIB),
        cost_estimate=pl.CostEstimate(
            flops=2 * total * depth * units * count,
            bytes_accessed=2 * (units * depth * count + total * units * count + total * depth),
            transcendentals=0,
        ),
        name="hidden_grad_partials",
    )(ids, *pieces, in_hbm(weight))


def filled(before):
    before = list(before or [])
    return before, [pl.BlockSpec(memory_space=pl.ANY)] * len(before)


def row_blocks(me, n):
    half = n // 2
    left = me < half
    place = jnp.where(left, me, n - 1 - me)
    near = [lax.rem(place + step, half) for step in range(half)]
    near = [jnp.where(left, at, n - 1 - at) for at in near]
    far = [jnp.where(left, n - 1 - at, at) for at in reversed(range(half))]
    return near + far


def factor_kernel(n, count, ids, *refs):
    sources, outs = refs[:-3], refs[-3:]
    sources = list(sources)
    rows = sources[0].shape[0] // 2
    half = n // 2
    place = jnp.where(ids[0] < half, ids[0], n - 1 - ids[0])
    for number, inner in enumerate(count):
        block = sources.pop(0)[...]
        if inner is not None:
            block = jnp.where(place >= inner[0], block, sources.pop(0)[...])
        gate = block[:rows].astype(F32)
        up = block[rows:].astype(F32)
        sigma = 1.0 / (1.0 + jnp.exp(-gate))
        silu = gate * sigma
        part = pl.ds(number * rows, rows)
        outs[0][part, :] = (up * sigma * (1.0 + gate * (1.0 - sigma))).astype(BF16)
        outs[1][part, :] = silu.astype(BF16)
        outs[2][part, :] = (silu * up).astype(BF16)


def factors_of(ids, sources, n):
    operands, count = [], []
    for source in sources:
        if isinstance(source, tuple):
            inner, block, other = source
            operands += [block, other]
            count.append((inner,))
        else:
            operands.append(source)
            count.append(None)
    rows, width = operands[0].shape
    rows = rows // 2 * len(sources)
    tile = tile_of(width, 512)
    out = pl.BlockSpec((rows, tile), lambda j, *_: (0, j))
    return pl.pallas_call(
        functools.partial(factor_kernel, n, count),
        grid_spec=pltpu.PrefetchScalarGridSpec(
            num_scalar_prefetch=1,
            grid=(width // tile,),
            in_specs=[pl.BlockSpec((operands[0].shape[0], tile), lambda j, *_: (0, j))]
            * len(operands),
            out_specs=[out] * 3,
        ),
        out_shape=[jax.ShapeDtypeStruct((rows, width), BF16)] * 3,
        compiler_params=pltpu.CompilerParams(vmem_limit_bytes=16 * MIB),
        cost_estimate=pl.CostEstimate(
            flops=10 * rows * width,
            bytes_accessed=10 * rows * width * (8 if len(sources) == 1 else 1),
            transcendentals=rows * width,
        ),
        name="factors",
    )(ids, *operands)


def down_kernel(n, ids, early, late, cotangent, *refs):
    out, hidden = refs[-2:]
    rows = late.shape[0]
    for number, block in enumerate(row_blocks(ids[0], n)):
        source = late if number == n - 1 else early
        part = pl.ds(0 if number == n - 1 else number * rows, rows)
        hidden[rows_at(block * rows, rows), :] = source[part, :]
    out[...] = contract(hidden[...], cotangent[...], 0, 0).astype(BF16)


def down_grads(ids, early, late, cotangent, n, part, parts, before):
    total, depth = cotangent.shape
    width = late.shape[1]
    tile = tile_of(width // parts, 512)
    tiles = width // parts // tile
    more, more_specs = filled(before)
    return pl.pallas_call(
        functools.partial(down_kernel, n),
        grid_spec=pltpu.PrefetchScalarGridSpec(
            num_scalar_prefetch=1,
            grid=(tiles,),
            in_specs=[
                pl.BlockSpec((early.shape[0], tile), lambda j, *_: (0, part * tiles + j)),
                pl.BlockSpec((late.shape[0], tile), lambda j, *_: (0, part * tiles + j)),
                whole((total, depth)),
            ]
            + more_specs,
            out_specs=pl.BlockSpec((tile, depth), lambda j, *_: (part * tiles + j, 0)),
            scratch_shapes=[pltpu.VMEM((total, tile), BF16)],
        ),
        out_shape=jax.ShapeDtypeStruct((width, depth), BF16),
        input_output_aliases={4: 0} if more else {},
        compiler_params=pltpu.CompilerParams(vmem_limit_bytes=20 * MIB),
        cost_estimate=pl.CostEstimate(
            flops=2 * total * depth * width // parts,
            bytes_accessed=2 * (width * depth // parts + total * depth + total * width // parts),
            transcendentals=0,
        ),
        name="down_grad",
    )(ids, early, late, cotangent, *more)


def delta_kernel(n, n_col, first, last, ids, *refs):
    middle, got, *factors, gate_weight, up_weight = refs[:8]
    refs = list(refs[8:])
    before = None if first else refs.pop(0)
    if last:
        gate_out, up_out = refs[:2]
    else:
        inputs = refs.pop(0)
        running, gate_grad, up_grad, gate_out, up_out = refs[-5:]

    @pl.when(pl.program_id(0) == 0)
    def _():
        outer = jnp.logical_or(ids[0] == 0, ids[0] == n - 1)
        rows = middle.shape[0] // n
        for number, block in enumerate(row_blocks(ids[0], n)):
            part = rows_at(block * rows, rows)
            grad = jnp.where(outer, got[part, :], middle[part, :]).astype(F32)
            late = number == n - 1
            source = pl.ds(0 if late else number * rows, rows)
            gate_factor, up_factor = factors[2:] if late else factors[:2]
            gate_out[part, :] = (grad * gate_factor[source, :].astype(F32)).astype(BF16)
            up_out[part, :] = (grad * up_factor[source, :].astype(F32)).astype(BF16)

    term = contract(gate_out[...], gate_weight[...], 1, 1) + contract(
        up_out[...], up_weight[...], 1, 1
    )
    if not first:
        term += before[...]
    if not last:
        running[...] = term
        gate_grad[...] = contract(inputs[...], gate_out[...], 1, 0).astype(BF16)
        up_grad[...] = contract(inputs[...], up_out[...], 1, 0).astype(BF16)
        return
    keep, send, result = refs[2:]
    result[...] = term
    rows = keep.shape[1]
    for slot in range(n_col):
        out = send if slot % 2 else keep
        start = jnp.bitwise_xor(ids[1], slot) * rows
        out[slot // 2] = result[rows_at(start, rows), :].astype(BF16)


def deltas(ids, grads, factors, weights, inputs_t, n, n_col, chunk, before, weight_out):
    total, units = grads[0].shape
    depth, width = weights[0].shape
    rows = total // n_col
    tile = tile_of(depth, 512)
    tall = whole((total, units))
    wide = pl.BlockSpec((tile, units), lambda j, *_: (j, chunk))
    running = pl.BlockSpec((total, tile), lambda j, *_: (0, j))
    delta_shape = (total, units)
    last = chunk == CHUNKS - 1
    more = [] if before is None else [before]
    more_specs = [running] * len(more)
    aliases = {}
    if last:
        half = pl.BlockSpec((n_col // 2, rows, tile), lambda j, *_: (0, 0, j))
        out_specs = [tall, tall, half, half]
        out_shape = [jax.ShapeDtypeStruct(delta_shape, BF16)] * 2
        out_shape += [jax.ShapeDtypeStruct((n_col // 2, rows, depth), BF16)] * 2
        scratch = [pltpu.VMEM((total, tile), F32)]
    else:
        more.append(inputs_t)
        more_specs.append(pl.BlockSpec((tile, total), lambda j, *_: (j, 0)))
        held, held_specs = filled(weight_out)
        aliases = {9 + len(more) + number: 1 + number for number in range(len(held))}
        more += held
        more_specs += held_specs
        out_specs = [running, wide, wide]
        out_shape = [jax.ShapeDtypeStruct((total, depth), F32)]
        out_shape += [jax.ShapeDtypeStruct((depth, width), BF16)] * 2
        scratch = [pltpu.VMEM(delta_shape, BF16)] * 2
    factor_specs = [
        pl.BlockSpec((factor.shape[0], units), lambda j, *_: (0, chunk)) for factor in factors
    ]
    return pl.pallas_call(
        functools.partial(delta_kernel, n, n_col, before is None, last),
        grid_spec=pltpu.PrefetchScalarGridSpec(
            num_scalar_prefetch=1,
            grid=(depth // tile,),
            in_specs=[tall] * 2 + factor_specs + [wide] * 2 + more_specs,
            out_specs=out_specs,
            scratch_shapes=scratch,
        ),
        out_shape=out_shape,
        input_output_aliases=aliases,
        compiler_params=pltpu.CompilerParams(vmem_limit_bytes=28 * MIB),
        cost_estimate=NO_COST,
        name="chunk",
    )(ids, *grads, *factors, *weights, *more)


def weight_grad_kernel(inputs, gate_delta, up_delta, *refs):
    gate_out, up_out = refs[-2:]
    gate_out[...] = contract(inputs[...], gate_delta[...], 1, 0).astype(BF16)
    up_out[...] = contract(inputs[...], up_delta[...], 1, 0).astype(BF16)


def weight_grads(inputs_t, gate_delta, up_delta, chunk, before):
    depth, total = inputs_t.shape
    units = gate_delta.shape[1]
    tile = tile_of(depth, 512)
    more, more_specs = filled(before)
    out = pl.BlockSpec((tile, units), lambda j: (j, chunk))
    cost = NO_COST
    if chunk == CHUNKS - 1:
        cost = pl.CostEstimate(
            flops=4 * total * depth * units,
            bytes_accessed=4 * units * depth + 4 * total * units + 2 * total * depth,
            transcendentals=0,
        )
    return pl.pallas_call(
        weight_grad_kernel,
        grid=(depth // tile,),
        in_specs=[pl.BlockSpec((tile, total), lambda j: (j, 0))]
        + [whole((total, units))] * 2
        + more_specs,
        out_specs=[out, out],
        out_shape=[jax.ShapeDtypeStruct((depth, units * CHUNKS), BF16)] * 2,
        input_output_aliases={3: 0, 4: 1} if more else {},
        compiler_params=pltpu.CompilerParams(vmem_limit_bytes=16 * MIB),
        cost_estimate=cost,
        name="gate_and_up_grad",
    )(inputs_t, gate_delta, up_delta, *more)


def add(left, right):
    return (left.astype(F32) + right.astype(F32)).astype(BF16)


def on_device(
    n_row, n_col, inputs, cotangent, gate_pre, up_pre, gate_weight, up_weight, down_weight
):
    me = lax.axis_index("row")
    ids = jnp.stack([me, lax.axis_index("col")]).astype(jnp.int32)
    half = n_row // 2
    place = jnp.where(me < half, me, n_row - 1 - me)

    pre, token_block = joined((gate_pre, up_pre), (cotangent, inputs))
    ins, outs = own_half(pre, n_row)
    sources = [pre]
    for step in range(1, half):
        sources.append(outs[step] if half == 2 else (half - step, ins[half - step], outs[step]))
    far = [lax.ppermute(block, "row", across(n_row)) for block in ins]
    away = [sent_out(block, place, n_row) for block in far]
    sources += [(1, *pair) for pair in away]

    pieces = cube_gather(token_block, n_col)
    term, tokens = partials(ids, pieces, down_weight, 0, 1)
    tokens = after(tokens, ins[-1], far[0])
    terms = [term, *partials(ids, [tokens], down_weight, 1, CHUNKS - 1)]
    inputs_t = transpose(ids, pieces)

    early = factors_of(ids, sources[:-1], n_row)
    late = factors_of(ids, sources[-1:], n_row)
    factors = [*early[:2], *late[:2]]
    before = {0: [*early, *late]}
    running = weight_out = met = None
    sent = []

    def work_on(chunk, running, weight_out):
        made = deltas(
            ids,
            sent[chunk],
            factors,
            (gate_weight, up_weight),
            inputs_t,
            n_row,
            n_col,
            chunk,
            running,
            weight_out,
        )
        if chunk < CHUNKS - 1:
            running, *weight_out = lax.optimization_barrier(tuple(made))
            return running, weight_out
        gate_delta, up_delta, *running = made
        return running, weight_grads(inputs_t, gate_delta, up_delta, chunk, weight_out)

    for chunk, held in enumerate(terms):
        for step in range(half - 1):
            if met is not None:
                held = after(held, met, *([inputs_t] if chunk == 1 else []))
            got = lax.ppermute(held, "row", inward([step], n_row))
            met = got
            if chunk == 0:
                got = after(got, terms[-1], far[-1], away[0][1], inputs_t)
            held = add(held, got)
        if chunk == 1:
            held = after(held, crossed)
        got = crossed = lax.ppermute(held, "row", across(n_row))
        if chunk == CHUNKS - 1:
            hidden = after(late[2], sent[2][0])
            down_grad = down_grads(ids, early[2], hidden, tokens, n_row, 0, 2, None)
            got_0, down_grad = lax.optimization_barrier((sent[0][1], down_grad))
            sent[0] = (sent[0][0], got_0)
            running, weight_out = work_on(0, None, None)
            got, running, *weight_out = lax.optimization_barrier((got, running, *weight_out))
        elif chunk in before:
            got = after(got, *before[chunk])
        held = add(held, got)
        sent.append(sent_out(held, place, n_row))

    for chunk in range(1, CHUNKS):
        running, weight_out = work_on(chunk, running, weight_out)
    gate_grad, up_grad = weight_out
    keep, send = running
    hidden = after(late[2], send)
    down_grad = down_grads(ids, early[2], hidden, tokens, n_row, 1, 2, [down_grad])

    keep = add(keep, lax.ppermute(send, "col", [(i, i ^ 1) for i in range(n_col)]))
    input_grad = keep[0].astype(F32)
    for number in range(1, n_col // 2):
        pairs = [(i, i ^ (2 * number)) for i in range(n_col)]
        input_grad += lax.ppermute(keep[number], "col", pairs).astype(F32)
    input_grad = input_grad.astype(BF16)
    return (input_grad, gate_grad, up_grad, down_grad)


def solution(mesh):
    placed = (
        P("col", "row"),
        P("col", "row"),
        P("row", "col"),
        P("row", "col"),
        P("row", "col"),
        P("row", "col"),
        P("col", "row"),
    )
    return jax.shard_map(
        functools.partial(on_device, mesh.shape["row"], mesh.shape["col"]),
        mesh=mesh,
        in_specs=placed,
        out_specs=(P("col", "row"), P("row", "col"), P("row", "col"), P("col", "row")),
        check_vma=False,
    )
```

```python
import functools

import jax
import jax.numpy as jnp
from jax import lax
from jax.experimental import pallas as pl
from jax.experimental.pallas import tpu as pltpu
from jax.sharding import PartitionSpec as P

F32 = jnp.float32
BF16 = jnp.bfloat16
MIB = 1024 * 1024
NO_COST = pl.CostEstimate(flops=0, bytes_accessed=0, transcendentals=0)
CHUNKS = 4


def contract(left, right, left_dim, right_dim):
    return lax.dot_general(
        left, right, (((left_dim,), (right_dim,)), ((), ())), preferred_element_type=F32
    )


def whole(shape):
    return pl.BlockSpec(shape, lambda *_: (0,) * len(shape))


def tile_of(size, most):
    tile = min(size, most)
    while size % tile:
        tile //= 2
    return tile


def after(value, *others):
    return lax.optimization_barrier((value, *others))[0]


def inward(places, n):
    return [pair for p in places for pair in ((p, p + 1), (n - 1 - p, n - 2 - p))]


def outward(places, n):
    return [(target, source) for source, target in inward(places, n)]


def across(n):
    return [(n // 2 - 1, n // 2), (n // 2, n // 2 - 1)]


def own_half(block, n):
    half = n // 2
    ins, outs = [block], [block]
    for step in range(1, half):
        if half == 2:
            met = lax.ppermute(block, "row", inward([0], n) + outward([0], n))
            ins.append(met)
            outs.append(met)
        else:
            ins.append(lax.ppermute(ins[-1], "row", inward(range(step - 1, half - 1), n)))
            outs.append(lax.ppermute(outs[-1], "row", outward(range(half - step), n)))
    return ins, outs


def sent_out(block, place, n):
    got = block
    for step in reversed(range(n // 2 - 1)):
        if step < n // 2 - 2:
            block = jnp.where(place == step + 1, got, block)
        got = lax.ppermute(block, "row", outward([step], n))
    return block, got


def cube_bits(n):
    bits, bit = [], 1
    while bit < n:
        bits.append(bit)
        bit *= 2
    return bits


def cube_gather(block, n):
    pieces = {0: block}
    for bit in reversed(cube_bits(n)):
        pairs = [(i, i ^ bit) for i in range(n)]
        for slot in list(pieces):
            pieces[slot | bit] = lax.ppermute(pieces[slot], "col", pairs)
    return [pieces[k] for k in range(n)]


def rows_at(start, rows):
    return pl.ds(pl.multiple_of(start, 16), rows)


def spread(pieces, col, which, target):
    for slot, piece in enumerate(pieces):
        rows = piece.shape[0] // 2
        block = piece[which * rows : (which + 1) * rows, :]
        target[rows_at(jnp.bitwise_xor(col, slot) * rows, rows), :] = block


def in_hbm(array):
    return pltpu.with_memory_space_constraint(array, pltpu.HBM)


def join_kernel(*refs):
    arrived = refs[-1]
    count = len(refs) // 3
    copies = []
    for number, block in enumerate(refs[: 2 * count]):
        rows = block.shape[0]
        target = refs[2 * count + number // 2].at[pl.ds(number % 2 * rows, rows)]
        copies.append(pltpu.make_async_copy(block, target, arrived.at[number]))
    for copy in copies:
        copy.start()
    for copy in copies:
        copy.wait()


def joined(*pairs):
    blocks = [in_hbm(block) for pair in pairs for block in pair]
    return pl.pallas_call(
        join_kernel,
        in_specs=[pl.BlockSpec(memory_space=pl.ANY)] * len(blocks),
        out_specs=[pl.BlockSpec(memory_space=pltpu.VMEM)] * len(pairs),
        out_shape=[
            jax.ShapeDtypeStruct((2 * first.shape[0], first.shape[1]), first.dtype)
            for first, _ in pairs
        ],
        scratch_shapes=[pltpu.SemaphoreType.DMA((len(blocks),))],
        compiler_params=pltpu.CompilerParams(vmem_limit_bytes=16 * MIB),
        cost_estimate=pl.CostEstimate(
            flops=0,
            bytes_accessed=sum(8 * first.size for first, _ in pairs),
            transcendentals=0,
        ),
        name="join",
    )(*blocks)


def transpose_kernel(n_col, ids, *refs):
    pieces, (out, held) = refs[:n_col], refs[n_col:]
    spread(pieces, ids[1], 1, held)
    out[...] = held[...].T


def transpose(ids, pieces):
    n_col = len(pieces)
    rows, depth = pieces[0].shape
    total = rows // 2 * n_col
    return pl.pallas_call(
        functools.partial(transpose_kernel, n_col),
        grid_spec=pltpu.PrefetchScalarGridSpec(
            num_scalar_prefetch=1,
            grid=(1,),
            in_specs=[whole((rows, depth))] * n_col,
            out_specs=whole((depth, total)),
            scratch_shapes=[pltpu.VMEM((total, depth), BF16)],
        ),
        out_shape=jax.ShapeDtypeStruct((depth, total), BF16),
        compiler_params=pltpu.CompilerParams(vmem_limit_bytes=16 * MIB),
        cost_estimate=pl.CostEstimate(
            flops=0, bytes_accessed=4 * total * depth, transcendentals=0
        ),
        name="inputs_transposed",
    )(ids, *pieces)


def partial_kernel(n_pieces, ids, *refs):
    pieces, weight, refs = refs[:n_pieces], refs[n_pieces], refs[n_pieces + 1 :]
    if n_pieces > 1:
        *outs, tokens = refs

        @pl.when(pl.program_id(0) == 0)
        def _():
            spread(pieces, ids[1], 0, tokens)
    else:
        tokens, outs = pieces[0], refs
    term = contract(tokens[...], weight[...], 1, 1).astype(BF16)
    for number, out in enumerate(outs):

        @pl.when(pl.program_id(0) == number)
        def _():
            out[...] = term


def partials(ids, pieces, weight, first, count):
    rows, depth = pieces[0].shape
    total = rows * len(pieces) // (2 if len(pieces) > 1 else 1)
    units = weight.shape[0] // CHUNKS
    shapes = [(total, units)] * count
    if len(pieces) > 1:
        shapes.append((total, depth))
    return pl.pallas_call(
        functools.partial(partial_kernel, len(pieces)),
        grid_spec=pltpu.PrefetchScalarGridSpec(
            num_scalar_prefetch=1,
            grid=(count,),
            in_specs=[whole((rows, depth))] * len(pieces)
            + [pl.BlockSpec((units, depth), lambda j, *_: (first + j, 0))],
            out_specs=[whole(shape) for shape in shapes],
        ),
        out_shape=[jax.ShapeDtypeStruct(shape, BF16) for shape in shapes],
        compiler_params=pltpu.CompilerParams(vmem_limit_bytes=16 * MIB),
        cost_estimate=pl.CostEstimate(
            flops=2 * total * depth * units * count,
            bytes_accessed=2 * (units * depth * count + total * units * count + total * depth),
            transcendentals=0,
        ),
        name="hidden_grad_partials",
    )(ids, *pieces, in_hbm(weight))


def filled(before):
    before = list(before or [])
    return before, [pl.BlockSpec(memory_space=pl.ANY)] * len(before)


def row_blocks(me, n):
    half = n // 2
    left = me < half
    place = jnp.where(left, me, n - 1 - me)
    near = [lax.rem(place + step, half) for step in range(half)]
    near = [jnp.where(left, at, n - 1 - at) for at in near]
    far = [jnp.where(left, n - 1 - at, at) for at in reversed(range(half))]
    return near + far


def factor_kernel(n, count, ids, *refs):
    sources, outs = refs[:-3], refs[-3:]
    sources = list(sources)
    rows = sources[0].shape[0] // 2
    half = n // 2
    place = jnp.where(ids[0] < half, ids[0], n - 1 - ids[0])
    for number, inner in enumerate(count):
        block = sources.pop(0)[...]
        if inner is not None:
            block = jnp.where(place >= inner[0], block, sources.pop(0)[...])
        gate = block[:rows].astype(F32)
        up = block[rows:].astype(F32)
        sigma = 1.0 / (1.0 + jnp.exp(-gate))
        silu = gate * sigma
        part = pl.ds(number * rows, rows)
        outs[0][part, :] = (up * sigma * (1.0 + gate * (1.0 - sigma))).astype(BF16)
        outs[1][part, :] = silu.astype(BF16)
        outs[2][part, :] = (silu * up).astype(BF16)


def factors_of(ids, sources, n):
    operands, count = [], []
    for source in sources:
        if isinstance(source, tuple):
            inner, block, other = source
            operands += [block, other]
            count.append((inner,))
        else:
            operands.append(source)
            count.append(None)
    rows, width = operands[0].shape
    rows = rows // 2 * len(sources)
    tile = tile_of(width, 512)
    out = pl.BlockSpec((rows, tile), lambda j, *_: (0, j))
    return pl.pallas_call(
        functools.partial(factor_kernel, n, count),
        grid_spec=pltpu.PrefetchScalarGridSpec(
            num_scalar_prefetch=1,
            grid=(width // tile,),
            in_specs=[pl.BlockSpec((operands[0].shape[0], tile), lambda j, *_: (0, j))]
            * len(operands),
            out_specs=[out] * 3,
        ),
        out_shape=[jax.ShapeDtypeStruct((rows, width), BF16)] * 3,
        compiler_params=pltpu.CompilerParams(vmem_limit_bytes=16 * MIB),
        cost_estimate=pl.CostEstimate(
            flops=10 * rows * width,
            bytes_accessed=10 * rows * width * (8 if len(sources) == 1 else 1),
            transcendentals=rows * width,
        ),
        name="factors",
    )(ids, *operands)


def down_kernel(n, ids, early, late, cotangent, *refs):
    out, hidden = refs[-2:]
    rows = late.shape[0]
    for number, block in enumerate(row_blocks(ids[0], n)):
        source = late if number == n - 1 else early
        part = pl.ds(0 if number == n - 1 else number * rows, rows)
        hidden[rows_at(block * rows, rows), :] = source[part, :]
    out[...] = contract(hidden[...], cotangent[...], 0, 0).astype(BF16)


def down_grads(ids, early, late, cotangent, n, part, parts, before):
    total, depth = cotangent.shape
    width = late.shape[1]
    tile = tile_of(width // parts, 512)
    tiles = width // parts // tile
    more, more_specs = filled(before)
    return pl.pallas_call(
        functools.partial(down_kernel, n),
        grid_spec=pltpu.PrefetchScalarGridSpec(
            num_scalar_prefetch=1,
            grid=(tiles,),
            in_specs=[
                pl.BlockSpec((early.shape[0], tile), lambda j, *_: (0, part * tiles + j)),
                pl.BlockSpec((late.shape[0], tile), lambda j, *_: (0, part * tiles + j)),
                whole((total, depth)),
            ]
            + more_specs,
            out_specs=pl.BlockSpec((tile, depth), lambda j, *_: (part * tiles + j, 0)),
            scratch_shapes=[pltpu.VMEM((total, tile), BF16)],
        ),
        out_shape=jax.ShapeDtypeStruct((width, depth), BF16),
        input_output_aliases={4: 0} if more else {},
        compiler_params=pltpu.CompilerParams(vmem_limit_bytes=20 * MIB),
        cost_estimate=pl.CostEstimate(
            flops=2 * total * depth * width // parts,
            bytes_accessed=2 * (width * depth // parts + total * depth + total * width // parts),
            transcendentals=0,
        ),
        name="down_grad",
    )(ids, early, late, cotangent, *more)


def delta_kernel(n, n_col, first, last, ids, *refs):
    middle, got, *factors, gate_weight, up_weight = refs[:8]
    refs = list(refs[8:])
    before = None if first else refs.pop(0)
    if last:
        gate_out, up_out = refs[:2]
    else:
        inputs = refs.pop(0)
        running, gate_grad, up_grad, gate_out, up_out = refs[-5:]

    @pl.when(pl.program_id(0) == 0)
    def _():
        outer = jnp.logical_or(ids[0] == 0, ids[0] == n - 1)
        rows = middle.shape[0] // n
        for number, block in enumerate(row_blocks(ids[0], n)):
            part = rows_at(block * rows, rows)
            grad = jnp.where(outer, got[part, :], middle[part, :]).astype(F32)
            late = number == n - 1
            source = pl.ds(0 if late else number * rows, rows)
            gate_factor, up_factor = factors[2:] if late else factors[:2]
            gate_out[part, :] = (grad * gate_factor[source, :].astype(F32)).astype(BF16)
            up_out[part, :] = (grad * up_factor[source, :].astype(F32)).astype(BF16)

    term = contract(gate_out[...], gate_weight[...], 1, 1) + contract(
        up_out[...], up_weight[...], 1, 1
    )
    if not first:
        term += before[...]
    if not last:
        running[...] = term
        gate_grad[...] = contract(inputs[...], gate_out[...], 1, 0).astype(BF16)
        up_grad[...] = contract(inputs[...], up_out[...], 1, 0).astype(BF16)
        return
    keep, send, result = refs[2:]
    result[...] = term
    rows = keep.shape[1]
    for slot in range(n_col):
        out = send if slot % 2 else keep
        start = jnp.bitwise_xor(ids[1], slot) * rows
        out[slot // 2] = result[rows_at(start, rows), :].astype(BF16)


def deltas(ids, grads, factors, weights, inputs_t, n, n_col, chunk, before, weight_out):
    total, units = grads[0].shape
    depth, width = weights[0].shape
    rows = total // n_col
    tile = tile_of(depth, 768)
    tall = whole((total, units))
    wide = pl.BlockSpec((tile, units), lambda j, *_: (j, chunk))
    running = pl.BlockSpec((total, tile), lambda j, *_: (0, j))
    delta_shape = (total, units)
    last = chunk == CHUNKS - 1
    more = [] if before is None else [before]
    more_specs = [running] * len(more)
    aliases = {}
    if last:
        half = pl.BlockSpec((n_col // 2, rows, tile), lambda j, *_: (0, 0, j))
        out_specs = [tall, tall, half, half]
        out_shape = [jax.ShapeDtypeStruct(delta_shape, BF16)] * 2
        out_shape += [jax.ShapeDtypeStruct((n_col // 2, rows, depth), BF16)] * 2
        scratch = [pltpu.VMEM((total, tile), F32)]
    else:
        more.append(inputs_t)
        more_specs.append(pl.BlockSpec((tile, total), lambda j, *_: (j, 0)))
        held, held_specs = filled(weight_out)
        aliases = {9 + len(more) + number: 1 + number for number in range(len(held))}
        more += held
        more_specs += held_specs
        out_specs = [running, wide, wide]
        out_shape = [jax.ShapeDtypeStruct((total, depth), F32)]
        out_shape += [jax.ShapeDtypeStruct((depth, width), BF16)] * 2
        scratch = [pltpu.VMEM(delta_shape, BF16)] * 2
    factor_specs = [
        pl.BlockSpec((factor.shape[0], units), lambda j, *_: (0, chunk)) for factor in factors
    ]
    return pl.pallas_call(
        functools.partial(delta_kernel, n, n_col, before is None, last),
        grid_spec=pltpu.PrefetchScalarGridSpec(
            num_scalar_prefetch=1,
            grid=(depth // tile,),
            in_specs=[tall] * 2 + factor_specs + [wide] * 2 + more_specs,
            out_specs=out_specs,
            scratch_shapes=scratch,
        ),
        out_shape=out_shape,
        input_output_aliases=aliases,
        compiler_params=pltpu.CompilerParams(vmem_limit_bytes=28 * MIB),
        cost_estimate=NO_COST,
        name="chunk",
    )(ids, *grads, *factors, *weights, *more)


def weight_grad_kernel(inputs, gate_delta, up_delta, *refs):
    gate_out, up_out = refs[-2:]
    gate_out[...] = contract(inputs[...], gate_delta[...], 1, 0).astype(BF16)
    up_out[...] = contract(inputs[...], up_delta[...], 1, 0).astype(BF16)


def weight_grads(inputs_t, gate_delta, up_delta, chunk, before):
    depth, total = inputs_t.shape
    units = gate_delta.shape[1]
    tile = tile_of(depth, 768)
    more, more_specs = filled(before)
    out = pl.BlockSpec((tile, units), lambda j: (j, chunk))
    cost = NO_COST
    if chunk == CHUNKS - 1:
        cost = pl.CostEstimate(
            flops=4 * total * depth * units,
            bytes_accessed=4 * units * depth + 4 * total * units + 2 * total * depth,
            transcendentals=0,
        )
    return pl.pallas_call(
        weight_grad_kernel,
        grid=(depth // tile,),
        in_specs=[pl.BlockSpec((tile, total), lambda j: (j, 0))]
        + [whole((total, units))] * 2
        + more_specs,
        out_specs=[out, out],
        out_shape=[jax.ShapeDtypeStruct((depth, units * CHUNKS), BF16)] * 2,
        input_output_aliases={3: 0, 4: 1} if more else {},
        compiler_params=pltpu.CompilerParams(vmem_limit_bytes=16 * MIB),
        cost_estimate=cost,
        name="gate_and_up_grad",
    )(inputs_t, gate_delta, up_delta, *more)


def add(left, right):
    return (left.astype(F32) + right.astype(F32)).astype(BF16)


def on_device(
    n_row, n_col, inputs, cotangent, gate_pre, up_pre, gate_weight, up_weight, down_weight
):
    me = lax.axis_index("row")
    ids = jnp.stack([me, lax.axis_index("col")]).astype(jnp.int32)
    half = n_row // 2
    place = jnp.where(me < half, me, n_row - 1 - me)

    pre, token_block = joined((gate_pre, up_pre), (cotangent, inputs))
    ins, outs = own_half(pre, n_row)
    sources = [pre]
    for step in range(1, half):
        sources.append(outs[step] if half == 2 else (half - step, ins[half - step], outs[step]))
    far = [lax.ppermute(block, "row", across(n_row)) for block in ins]
    away = [sent_out(block, place, n_row) for block in far]
    sources += [(1, *pair) for pair in away]

    pieces = cube_gather(token_block, n_col)
    term, tokens = partials(ids, pieces, down_weight, 0, 1)
    tokens = after(tokens, ins[-1], far[0])
    terms = [term, *partials(ids, [tokens], down_weight, 1, CHUNKS - 1)]
    inputs_t = transpose(ids, pieces)

    early = factors_of(ids, sources[:-1], n_row)
    late = factors_of(ids, sources[-1:], n_row)
    factors = [*early[:2], *late[:2]]
    before = {0: [*early, *late]}
    running = weight_out = met = None
    sent = []

    def work_on(chunk, running, weight_out):
        made = deltas(
            ids,
            sent[chunk],
            factors,
            (gate_weight, up_weight),
            inputs_t,
            n_row,
            n_col,
            chunk,
            running,
            weight_out,
        )
        if chunk < CHUNKS - 1:
            running, *weight_out = lax.optimization_barrier(tuple(made))
            return running, weight_out
        gate_delta, up_delta, *running = made
        return running, weight_grads(inputs_t, gate_delta, up_delta, chunk, weight_out)

    for chunk, held in enumerate(terms):
        for step in range(half - 1):
            if met is not None:
                held = after(held, met, *([inputs_t] if chunk == 1 else []))
            got = lax.ppermute(held, "row", inward([step], n_row))
            met = got
            if chunk == 0:
                got = after(got, terms[-1], far[-1], away[0][1], inputs_t)
            held = add(held, got)
        if chunk == 1:
            held = after(held, crossed)
        got = crossed = lax.ppermute(held, "row", across(n_row))
        if chunk == CHUNKS - 1:
            hidden = after(late[2], sent[2][0])
            down_grad = down_grads(ids, early[2], hidden, tokens, n_row, 0, 2, None)
            got_0, down_grad = lax.optimization_barrier((sent[0][1], down_grad))
            sent[0] = (sent[0][0], got_0)
            running, weight_out = work_on(0, None, None)
            got, running, *weight_out = lax.optimization_barrier((got, running, *weight_out))
        elif chunk in before:
            got = after(got, *before[chunk])
        held = add(held, got)
        sent.append(sent_out(held, place, n_row))

    for chunk in range(1, CHUNKS):
        running, weight_out = work_on(chunk, running, weight_out)
    gate_grad, up_grad = weight_out
    keep, send = running
    hidden = after(late[2], send)
    down_grad = down_grads(ids, early[2], hidden, tokens, n_row, 1, 2, [down_grad])

    keep = add(keep, lax.ppermute(send, "col", [(i, i ^ 1) for i in range(n_col)]))
    input_grad = keep[0].astype(F32)
    for number in range(1, n_col // 2):
        pairs = [(i, i ^ (2 * number)) for i in range(n_col)]
        input_grad += lax.ppermute(keep[number], "col", pairs).astype(F32)
    input_grad = input_grad.astype(BF16)
    return (input_grad, gate_grad, up_grad, down_grad)


def solution(mesh):
    placed = (
        P("col", "row"),
        P("col", "row"),
        P("row", "col"),
        P("row", "col"),
        P("row", "col"),
        P("row", "col"),
        P("col", "row"),
    )
    return jax.shard_map(
        functools.partial(on_device, mesh.shape["row"], mesh.shape["col"]),
        mesh=mesh,
        in_specs=placed,
        out_specs=(P("col", "row"), P("row", "col"), P("row", "col"), P("col", "row")),
        check_vma=False,
    )
```

```python
import functools

import jax
import jax.numpy as jnp
from jax import lax
from jax.experimental import pallas as pl
from jax.experimental.pallas import tpu as pltpu
from jax.sharding import PartitionSpec as P

F32 = jnp.float32
BF16 = jnp.bfloat16
MIB = 1024 * 1024
NO_COST = pl.CostEstimate(flops=0, bytes_accessed=0, transcendentals=0)
CHUNKS = 4


def contract(left, right, left_dim, right_dim):
    return lax.dot_general(
        left, right, (((left_dim,), (right_dim,)), ((), ())), preferred_element_type=F32
    )


def whole(shape):
    return pl.BlockSpec(shape, lambda *_: (0,) * len(shape))


def tile_of(size, most):
    tile = min(size, most)
    while size % tile:
        tile //= 2
    return tile


def after(value, *others):
    return lax.optimization_barrier((value, *others))[0]


def inward(places, n):
    return [pair for p in places for pair in ((p, p + 1), (n - 1 - p, n - 2 - p))]


def outward(places, n):
    return [(target, source) for source, target in inward(places, n)]


def across(n):
    return [(n // 2 - 1, n // 2), (n // 2, n // 2 - 1)]


def own_half(block, n):
    half = n // 2
    ins, outs = [block], [block]
    for step in range(1, half):
        if half == 2:
            met = lax.ppermute(block, "row", inward([0], n) + outward([0], n))
            ins.append(met)
            outs.append(met)
        else:
            ins.append(lax.ppermute(ins[-1], "row", inward(range(step - 1, half - 1), n)))
            outs.append(lax.ppermute(outs[-1], "row", outward(range(half - step), n)))
    return ins, outs


def sent_out(block, place, n):
    got = block
    for step in reversed(range(n // 2 - 1)):
        if step < n // 2 - 2:
            block = jnp.where(place == step + 1, got, block)
        got = lax.ppermute(block, "row", outward([step], n))
    return block, got


def cube_bits(n):
    bits, bit = [], 1
    while bit < n:
        bits.append(bit)
        bit *= 2
    return bits


def cube_gather(block, n):
    pieces = {0: block}
    for bit in reversed(cube_bits(n)):
        pairs = [(i, i ^ bit) for i in range(n)]
        for slot in list(pieces):
            pieces[slot | bit] = lax.ppermute(pieces[slot], "col", pairs)
    return [pieces[k] for k in range(n)]


def rows_at(start, rows):
    return pl.ds(pl.multiple_of(start, 16), rows)


def spread(pieces, col, which, target):
    for slot, piece in enumerate(pieces):
        rows = piece.shape[0] // 2
        block = piece[which * rows : (which + 1) * rows, :]
        target[rows_at(jnp.bitwise_xor(col, slot) * rows, rows), :] = block


def in_hbm(array):
    return pltpu.with_memory_space_constraint(array, pltpu.HBM)


def join_kernel(*refs):
    arrived = refs[-1]
    count = len(refs) // 3
    copies = []
    for number, block in enumerate(refs[: 2 * count]):
        rows = block.shape[0]
        target = refs[2 * count + number // 2].at[pl.ds(number % 2 * rows, rows)]
        copies.append(pltpu.make_async_copy(block, target, arrived.at[number]))
    for copy in copies:
        copy.start()
    for copy in copies:
        copy.wait()


def joined(*pairs):
    blocks = [in_hbm(block) for pair in pairs for block in pair]
    return pl.pallas_call(
        join_kernel,
        in_specs=[pl.BlockSpec(memory_space=pl.ANY)] * len(blocks),
        out_specs=[pl.BlockSpec(memory_space=pltpu.VMEM)] * len(pairs),
        out_shape=[
            jax.ShapeDtypeStruct((2 * first.shape[0], first.shape[1]), first.dtype)
            for first, _ in pairs
        ],
        scratch_shapes=[pltpu.SemaphoreType.DMA((len(blocks),))],
        compiler_params=pltpu.CompilerParams(vmem_limit_bytes=16 * MIB),
        cost_estimate=pl.CostEstimate(
            flops=0,
            bytes_accessed=sum(8 * first.size for first, _ in pairs),
            transcendentals=0,
        ),
        name="join",
    )(*blocks)


def transpose_kernel(n_col, ids, *refs):
    pieces, (out, held) = refs[:n_col], refs[n_col:]
    spread(pieces, ids[1], 1, held)
    out[...] = held[...].T


def transpose(ids, pieces):
    n_col = len(pieces)
    rows, depth = pieces[0].shape
    total = rows // 2 * n_col
    return pl.pallas_call(
        functools.partial(transpose_kernel, n_col),
        grid_spec=pltpu.PrefetchScalarGridSpec(
            num_scalar_prefetch=1,
            grid=(1,),
            in_specs=[whole((rows, depth))] * n_col,
            out_specs=whole((depth, total)),
            scratch_shapes=[pltpu.VMEM((total, depth), BF16)],
        ),
        out_shape=jax.ShapeDtypeStruct((depth, total), BF16),
        compiler_params=pltpu.CompilerParams(vmem_limit_bytes=16 * MIB),
        cost_estimate=pl.CostEstimate(
            flops=0, bytes_accessed=4 * total * depth, transcendentals=0
        ),
        name="inputs_transposed",
    )(ids, *pieces)


def partial_kernel(n_pieces, ids, *refs):
    pieces, weight, refs = refs[:n_pieces], refs[n_pieces], refs[n_pieces + 1 :]
    if n_pieces > 1:
        *outs, tokens = refs

        @pl.when(pl.program_id(0) == 0)
        def _():
            spread(pieces, ids[1], 0, tokens)
    else:
        tokens, outs = pieces[0], refs
    term = contract(tokens[...], weight[...], 1, 1).astype(BF16)
    for number, out in enumerate(outs):

        @pl.when(pl.program_id(0) == number)
        def _():
            out[...] = term


def partials(ids, pieces, weight, first, count):
    rows, depth = pieces[0].shape
    total = rows * len(pieces) // (2 if len(pieces) > 1 else 1)
    units = weight.shape[0] // CHUNKS
    shapes = [(total, units)] * count
    if len(pieces) > 1:
        shapes.append((total, depth))
    return pl.pallas_call(
        functools.partial(partial_kernel, len(pieces)),
        grid_spec=pltpu.PrefetchScalarGridSpec(
            num_scalar_prefetch=1,
            grid=(count,),
            in_specs=[whole((rows, depth))] * len(pieces)
            + [pl.BlockSpec((units, depth), lambda j, *_: (first + j, 0))],
            out_specs=[whole(shape) for shape in shapes],
        ),
        out_shape=[jax.ShapeDtypeStruct(shape, BF16) for shape in shapes],
        compiler_params=pltpu.CompilerParams(vmem_limit_bytes=16 * MIB),
        cost_estimate=pl.CostEstimate(
            flops=2 * total * depth * units * count,
            bytes_accessed=2 * (units * depth * count + total * units * count + total * depth),
            transcendentals=0,
        ),
        name="hidden_grad_partials",
    )(ids, *pieces, in_hbm(weight))


def filled(before):
    before = list(before or [])
    return before, [pl.BlockSpec(memory_space=pl.ANY)] * len(before)


def row_blocks(me, n):
    half = n // 2
    left = me < half
    place = jnp.where(left, me, n - 1 - me)
    near = [lax.rem(place + step, half) for step in range(half)]
    near = [jnp.where(left, at, n - 1 - at) for at in near]
    far = [jnp.where(left, n - 1 - at, at) for at in reversed(range(half))]
    return near + far


def factor_kernel(n, count, ids, *refs):
    sources, outs = refs[:-3], refs[-3:]
    sources = list(sources)
    rows = sources[0].shape[0] // 2
    half = n // 2
    place = jnp.where(ids[0] < half, ids[0], n - 1 - ids[0])
    for number, inner in enumerate(count):
        block = sources.pop(0)[...]
        if inner is not None:
            block = jnp.where(place >= inner[0], block, sources.pop(0)[...])
        gate = block[:rows].astype(F32)
        up = block[rows:].astype(F32)
        sigma = 1.0 / (1.0 + jnp.exp(-gate))
        silu = gate * sigma
        part = pl.ds(number * rows, rows)
        outs[0][part, :] = (up * sigma * (1.0 + gate * (1.0 - sigma))).astype(BF16)
        outs[1][part, :] = silu.astype(BF16)
        outs[2][part, :] = (silu * up).astype(BF16)


def factors_of(ids, sources, n):
    operands, count = [], []
    for source in sources:
        if isinstance(source, tuple):
            inner, block, other = source
            operands += [block, other]
            count.append((inner,))
        else:
            operands.append(source)
            count.append(None)
    rows, width = operands[0].shape
    rows = rows // 2 * len(sources)
    tile = tile_of(width, 512)
    out = pl.BlockSpec((rows, tile), lambda j, *_: (0, j))
    return pl.pallas_call(
        functools.partial(factor_kernel, n, count),
        grid_spec=pltpu.PrefetchScalarGridSpec(
            num_scalar_prefetch=1,
            grid=(width // tile,),
            in_specs=[pl.BlockSpec((operands[0].shape[0], tile), lambda j, *_: (0, j))]
            * len(operands),
            out_specs=[out] * 3,
        ),
        out_shape=[jax.ShapeDtypeStruct((rows, width), BF16)] * 3,
        compiler_params=pltpu.CompilerParams(vmem_limit_bytes=16 * MIB),
        cost_estimate=pl.CostEstimate(
            flops=10 * rows * width,
            bytes_accessed=10 * rows * width * (8 if len(sources) == 1 else 1),
            transcendentals=rows * width,
        ),
        name="factors",
    )(ids, *operands)


def down_kernel(n, ids, early, late, cotangent, *refs):
    out, hidden = refs[-2:]
    rows = late.shape[0]
    for number, block in enumerate(row_blocks(ids[0], n)):
        source = late if number == n - 1 else early
        part = pl.ds(0 if number == n - 1 else number * rows, rows)
        hidden[rows_at(block * rows, rows), :] = source[part, :]
    out[...] = contract(hidden[...], cotangent[...], 0, 0).astype(BF16)


def down_grads(ids, early, late, cotangent, n, part, parts, before):
    total, depth = cotangent.shape
    width = late.shape[1]
    tile = tile_of(width // parts, 512)
    tiles = width // parts // tile
    more, more_specs = filled(before)
    return pl.pallas_call(
        functools.partial(down_kernel, n),
        grid_spec=pltpu.PrefetchScalarGridSpec(
            num_scalar_prefetch=1,
            grid=(tiles,),
            in_specs=[
                pl.BlockSpec((early.shape[0], tile), lambda j, *_: (0, part * tiles + j)),
                pl.BlockSpec((late.shape[0], tile), lambda j, *_: (0, part * tiles + j)),
                whole((total, depth)),
            ]
            + more_specs,
            out_specs=pl.BlockSpec((tile, depth), lambda j, *_: (part * tiles + j, 0)),
            scratch_shapes=[pltpu.VMEM((total, tile), BF16)],
        ),
        out_shape=jax.ShapeDtypeStruct((width, depth), BF16),
        input_output_aliases={4: 0} if more else {},
        compiler_params=pltpu.CompilerParams(vmem_limit_bytes=20 * MIB),
        cost_estimate=pl.CostEstimate(
            flops=2 * total * depth * width // parts,
            bytes_accessed=2 * (width * depth // parts + total * depth + total * width // parts),
            transcendentals=0,
        ),
        name="down_grad",
    )(ids, early, late, cotangent, *more)


def delta_kernel(n, n_col, first, last, ids, *refs):
    middle, got, *factors, gate_weight, up_weight = refs[:8]
    refs = list(refs[8:])
    before = None if first else refs.pop(0)
    if last:
        gate_out, up_out = refs[:2]
    else:
        inputs = refs.pop(0)
        running, gate_grad, up_grad, gate_out, up_out = refs[-5:]

    @pl.when(pl.program_id(0) == 0)
    def _():
        outer = jnp.logical_or(ids[0] == 0, ids[0] == n - 1)
        rows = middle.shape[0] // n
        for number, block in enumerate(row_blocks(ids[0], n)):
            part = rows_at(block * rows, rows)
            grad = jnp.where(outer, got[part, :], middle[part, :]).astype(F32)
            late = number == n - 1
            source = pl.ds(0 if late else number * rows, rows)
            gate_factor, up_factor = factors[2:] if late else factors[:2]
            gate_out[part, :] = (grad * gate_factor[source, :].astype(F32)).astype(BF16)
            up_out[part, :] = (grad * up_factor[source, :].astype(F32)).astype(BF16)

    term = contract(gate_out[...], gate_weight[...], 1, 1) + contract(
        up_out[...], up_weight[...], 1, 1
    )
    if not first:
        term += before[...]
    if not last:
        running[...] = term
        gate_grad[...] = contract(inputs[...], gate_out[...], 1, 0).astype(BF16)
        up_grad[...] = contract(inputs[...], up_out[...], 1, 0).astype(BF16)
        return
    keep, send, result = refs[2:]
    result[...] = term
    rows = keep.shape[1]
    for slot in range(n_col):
        out = send if slot % 2 else keep
        start = jnp.bitwise_xor(ids[1], slot) * rows
        out[slot // 2] = result[rows_at(start, rows), :].astype(BF16)


def deltas(ids, grads, factors, weights, inputs_t, n, n_col, chunk, before, weight_out):
    total, units = grads[0].shape
    depth, width = weights[0].shape
    rows = total // n_col
    tile = tile_of(depth, 768)
    tall = whole((total, units))
    wide = pl.BlockSpec((tile, units), lambda j, *_: (j, chunk))
    running = pl.BlockSpec((total, tile), lambda j, *_: (0, j))
    delta_shape = (total, units)
    last = chunk == CHUNKS - 1
    more = [] if before is None else [before]
    more_specs = [running] * len(more)
    aliases = {}
    if last:
        half = pl.BlockSpec((n_col // 2, rows, tile), lambda j, *_: (0, 0, j))
        out_specs = [tall, tall, half, half]
        out_shape = [jax.ShapeDtypeStruct(delta_shape, BF16)] * 2
        out_shape += [jax.ShapeDtypeStruct((n_col // 2, rows, depth), BF16)] * 2
        scratch = [pltpu.VMEM((total, tile), F32)]
    else:
        more.append(inputs_t)
        more_specs.append(pl.BlockSpec((tile, total), lambda j, *_: (j, 0)))
        held, held_specs = filled(weight_out)
        aliases = {9 + len(more) + number: 1 + number for number in range(len(held))}
        more += held
        more_specs += held_specs
        out_specs = [running, wide, wide]
        out_shape = [jax.ShapeDtypeStruct((total, depth), F32)]
        out_shape += [jax.ShapeDtypeStruct((depth, width), BF16)] * 2
        scratch = [pltpu.VMEM(delta_shape, BF16)] * 2
    factor_specs = [
        pl.BlockSpec((factor.shape[0], units), lambda j, *_: (0, chunk)) for factor in factors
    ]
    return pl.pallas_call(
        functools.partial(delta_kernel, n, n_col, before is None, last),
        grid_spec=pltpu.PrefetchScalarGridSpec(
            num_scalar_prefetch=1,
            grid=(depth // tile,),
            in_specs=[tall] * 2 + factor_specs + [wide] * 2 + more_specs,
            out_specs=out_specs,
            scratch_shapes=scratch,
        ),
        out_shape=out_shape,
        input_output_aliases=aliases,
        compiler_params=pltpu.CompilerParams(vmem_limit_bytes=28 * MIB),
        cost_estimate=NO_COST,
        name="chunk",
    )(ids, *grads, *factors, *weights, *more)


def weight_grad_kernel(inputs, gate_delta, up_delta, *refs):
    gate_out, up_out = refs[-2:]
    gate_out[...] = contract(inputs[...], gate_delta[...], 1, 0).astype(BF16)
    up_out[...] = contract(inputs[...], up_delta[...], 1, 0).astype(BF16)


def weight_grads(inputs_t, gate_delta, up_delta, chunk, before):
    depth, total = inputs_t.shape
    units = gate_delta.shape[1]
    tile = tile_of(depth, 768)
    more, more_specs = filled(before)
    out = pl.BlockSpec((tile, units), lambda j: (j, chunk))
    cost = NO_COST
    if chunk == CHUNKS - 1:
        cost = pl.CostEstimate(
            flops=4 * total * depth * units,
            bytes_accessed=4 * units * depth + 4 * total * units + 2 * total * depth,
            transcendentals=0,
        )
    return pl.pallas_call(
        weight_grad_kernel,
        grid=(depth // tile,),
        in_specs=[pl.BlockSpec((tile, total), lambda j: (j, 0))]
        + [whole((total, units))] * 2
        + more_specs,
        out_specs=[out, out],
        out_shape=[jax.ShapeDtypeStruct((depth, units * CHUNKS), BF16)] * 2,
        input_output_aliases={3: 0, 4: 1} if more else {},
        compiler_params=pltpu.CompilerParams(vmem_limit_bytes=16 * MIB),
        cost_estimate=cost,
        name="gate_and_up_grad",
    )(inputs_t, gate_delta, up_delta, *more)


def add(left, right):
    return (left.astype(F32) + right.astype(F32)).astype(BF16)


def on_device(
    n_row, n_col, inputs, cotangent, gate_pre, up_pre, gate_weight, up_weight, down_weight
):
    me = lax.axis_index("row")
    ids = jnp.stack([me, lax.axis_index("col")]).astype(jnp.int32)
    half = n_row // 2
    place = jnp.where(me < half, me, n_row - 1 - me)

    pre, token_block = joined((gate_pre, up_pre), (cotangent, inputs))
    ins, outs = own_half(pre, n_row)
    sources = [pre]
    for step in range(1, half):
        sources.append(outs[step] if half == 2 else (half - step, ins[half - step], outs[step]))
    far = [lax.ppermute(block, "row", across(n_row)) for block in ins]
    away = [sent_out(block, place, n_row) for block in far]
    sources += [(1, *pair) for pair in away]

    pieces = cube_gather(token_block, n_col)
    term, tokens = partials(ids, pieces, down_weight, 0, 1)
    tokens = after(tokens, ins[-1], far[0])
    terms = [term, *partials(ids, [tokens], down_weight, 1, CHUNKS - 1)]
    inputs_t = transpose(ids, pieces)

    early = factors_of(ids, sources[:-1], n_row)
    late = factors_of(ids, sources[-1:], n_row)
    factors = [*early[:2], *late[:2]]
    before = {0: [*early, *late]}
    running = weight_out = met = None
    sent = []

    def work_on(chunk, running, weight_out):
        made = deltas(
            ids,
            sent[chunk],
            factors,
            (gate_weight, up_weight),
            inputs_t,
            n_row,
            n_col,
            chunk,
            running,
            weight_out,
        )
        if chunk < CHUNKS - 1:
            running, *weight_out = lax.optimization_barrier(tuple(made))
            return running, weight_out
        gate_delta, up_delta, *running = made
        return running, weight_grads(inputs_t, gate_delta, up_delta, chunk, weight_out)

    for chunk, held in enumerate(terms):
        for step in range(half - 1):
            if met is not None:
                held = after(held, met, *([inputs_t] if chunk == 1 else []))
            got = lax.ppermute(held, "row", inward([step], n_row))
            met = got
            if chunk == 0:
                got = after(got, terms[-1], far[-1], away[0][1], inputs_t)
            held = add(held, got)
        if chunk == 1:
            held = after(held, crossed)
        got = crossed = lax.ppermute(held, "row", across(n_row))
        if chunk == CHUNKS - 1:
            hidden = after(late[2], sent[2][0])
            down_grad = down_grads(ids, early[2], hidden, tokens, n_row, 0, 2, None)
            got_0, down_grad = lax.optimization_barrier((sent[0][1], down_grad))
            sent[0] = (sent[0][0], got_0)
            running, weight_out = work_on(0, None, None)
            got, running, *weight_out = lax.optimization_barrier((got, running, *weight_out))
        elif chunk in before:
            got = after(got, *before[chunk])
        held = add(held, got)
        sent.append(sent_out(held, place, n_row))

    for chunk in range(1, CHUNKS):
        if chunk == CHUNKS - 2:
            hidden = after(late[2], running)
            down_grad = down_grads(ids, early[2], hidden, tokens, n_row, 1, 2, [down_grad])
            running, down_grad = lax.optimization_barrier((running, down_grad))
        running, weight_out = work_on(chunk, running, weight_out)
    gate_grad, up_grad = weight_out
    keep, send = running

    keep = add(keep, lax.ppermute(send, "col", [(i, i ^ 1) for i in range(n_col)]))
    input_grad = keep[0].astype(F32)
    for number in range(1, n_col // 2):
        pairs = [(i, i ^ (2 * number)) for i in range(n_col)]
        input_grad += lax.ppermute(keep[number], "col", pairs).astype(F32)
    input_grad = input_grad.astype(BF16)
    return (input_grad, gate_grad, up_grad, down_grad)


def solution(mesh):
    placed = (
        P("col", "row"),
        P("col", "row"),
        P("row", "col"),
        P("row", "col"),
        P("row", "col"),
        P("row", "col"),
        P("col", "row"),
    )
    return jax.shard_map(
        functools.partial(on_device, mesh.shape["row"], mesh.shape["col"]),
        mesh=mesh,
        in_specs=placed,
        out_specs=(P("col", "row"), P("row", "col"), P("row", "col"), P("col", "row")),
        check_vma=False,
    )
```
